256 devices in a mesh: dp: 16 (over y, x), tensor: 16 (over z, core).
Axes of the slice: x: 4, y: 4, z: 8, core: 2. Of those that a mesh axis runs over, the one named last changes fastest.
Arguments:
- hidden_in: bfloat16 [32768, 8192], P('dp', 'tensor'), may hold values from -6 to 6
- grad_gate: bfloat16 [32768, 16384], P('dp', 'tensor'), may hold values from -6 to 6
- adapter_in: bfloat16 [64, 16, 8192], P('dp', None, 'tensor'), may hold values from -0.23925781 to 0.23925781
- adapter_out: bfloat16 [64, 16, 16384], P('dp', None, 'tensor'), may hold values from -0.046875 to 0.046875
- block_tenant: int32 [256], replicated, may hold values from 0 to 63
- block_dest: int32 [256, 1], replicated, may hold values from 0 to 15; in each aligned block of 16 rows (0 to 15, 16 to 31, ...) at most 2 rows name the same one
- tenant_tokens: int32 [64], replicated, may hold values from 128 to 1024
- tenant_owner: int32 [64], replicated, may hold values from 0 to 63, each once
Outputs:
- dgrad_placed: bfloat16 [65536, 8192], P('dp', 'tensor')
- grad_in: float32 [64, 16, 8192], P('dp', None, 'tensor')
- grad_out: float32 [64, 16, 16384], P('dp', None, 'tensor')
- tenant_norms: float32 [64], P('dp')
The draws below stay inside these ranges and needn't reach their ends.
Inputs may be any that keep to these rules, and one draw needn't show every extreme that they name: `block_dest`: among the 16 blocks of one data group (blocks g * 16 to g * 16 + 15) at most 2 name the same destination group, and in some data group exactly 2 name one destination. `tenant_owner`: A permutation: every row of 0 to 63 belongs to exactly one tenant.
All inputs are finite; a program needn't handle non-finite values.
Results may differ from the reference program's by a relative error of at most 0.0049.
Values may be sent and summed in bfloat16 or wider, within the bound.
A program may use at most 128 MiB of HBM per device.

```python
import math
import jax
import jax.numpy as jnp
import numpy as np
from jax import lax

D = 8192
FF = 16384
ADAPTER_RANK = 16
PLAN_BLOCK_ROWS = 128
BLK_G = 16
NBLK = 256
TOKENS = 32768
TEN = 64
SEND = 2
SLOTS = 32
N_DP = 16


def touch_ends(entries, rng, least, high):
    longest = entries.shape.index(max(entries.shape))
    spots = []
    for shift in (0, 1):
        where = [jax.random.randint(jax.random.fold_in(rng, axis), (), 0, length) for axis, length in enumerate(entries.shape)]
        where[longest] = (where[longest] + shift) % entries.shape[longest]
        spots.append(tuple(where))
    return entries.at[spots[0]].set(least).at[spots[1]].set(high)


def block_scale(rng, dims, cuts, low, top_value):
    def one(dim, blocks):
        draws = jax.random.uniform(jax.random.fold_in(jax.random.fold_in(rng, 6), dim), (blocks,), jnp.float32, low / len(cuts), top_value / len(cuts))
        return jnp.repeat(jnp.exp(draws), dims[dim] // blocks).reshape((-1,) + (1,) * (len(dims) - dim - 1))

    factor_of = one(*cuts[0])
    for cut in cuts[1:]:
        factor_of = factor_of * one(*cut)
    return factor_of


def rank_bounds(number_of, slope):
    weights = [(1 << 20) // math.isqrt(rank ** slope) + 1 for rank in range(1, number_of + 1)]
    deviation = 1 + sum(weights) // (1 << 30)
    return np.cumsum(np.array([max(1, weight // deviation) for weight in weights]))


def ranked(key, extent, amount, lean):
    listing = rank_bounds(amount, lean)
    pick = jax.random.randint(jax.random.fold_in(key, 1), extent, 0, int(listing[amount - 1]))
    rank = jnp.searchsorted(jnp.asarray(listing, jnp.int32), pick, side="right")
    return jax.random.permutation(jax.random.fold_in(key, 2), amount)[rank].astype(jnp.int32)


def deal_out(stream_key, own, number, rows, count, top, bound, slope):
    order = jax.random.permutation(stream_key, count)
    packed, ordinary = portions_of(count, rows * top, bound, slope, True), portions_of(count, rows * top, bound, slope, False)
    places = jnp.arange(count)

    def named(sizes, turn):
        used = int((sizes > 0).sum())
        fixed = max(1, used // 4)
        moved = fixed + (places - fixed + turn * (used - fixed)) % max(1, count - fixed)
        return jnp.zeros((count,), jnp.int32).at[order[jnp.where(places < fixed, places, moved)]].set(jnp.asarray(sizes, jnp.int32))

    sizes = jnp.where(number % 4 == 0, named(packed, number // 4), named(ordinary, number - number // 4 - 1))
    mixed = jax.random.permutation(jax.random.fold_in(own, 3), count)
    giver, sink = mixed[0:count // 2 * 2:2], mixed[1:count // 2 * 2:2]
    room = jnp.minimum(sizes[giver] - 1, bound - sizes[sink]) // 2
    room = jnp.where((giver == order[0]) | (sink == order[0]) | (sizes[sink] == 0), 0, jnp.maximum(room, 0))
    moved = jax.random.randint(jax.random.fold_in(own, 4), (count // 2,), 0, 1 << 20) % (room + 1)
    sizes = sizes.at[giver].add(-moved).at[sink].add(moved)
    items = jnp.searchsorted(jnp.cumsum(sizes), jnp.arange(rows * top), side="right").astype(jnp.int32)
    table = items.reshape(top, rows).T
    table = table[jax.random.permutation(jax.random.fold_in(own, 1), rows)]
    turn = jax.random.randint(jax.random.fold_in(own, 2), (rows, 1), 0, top)
    return jnp.take_along_axis(table, (jnp.arange(top)[None, :] + turn) % top, axis=1)


def portions_of(number_of, total, limit, slope, full):
    portions = [(1 << 20) // math.isqrt(standing ** slope) + 1 for standing in range(1, number_of + 1)]
    largest = limit if full else min(limit, max(-(-total // number_of), total * portions[0] // sum(portions)))
    least = 1 if total - largest >= number_of - 1 else 0
    counts, rest = [largest] + [least] * (number_of - 1), total - largest - least * (number_of - 1)
    while rest > 0:
        free = [i for i in range(1, number_of) if counts[i] < largest] or [i for i in range(1, number_of) if counts[i] < limit]
        mass, left = sum([portions[i] for i in free]), rest
        for i in free:
            more = min(limit - counts[i], max(1, left * portions[i] // mass), rest)
            counts[i] = counts[i] + more
            rest = rest - more
    return np.array(counts)


def bell_draw(key, shape, width, bound, pieces=(), kind=jnp.bfloat16):
    array = width * jax.random.normal(key, shape, jnp.float32)
    if pieces:
        array = array * block_scale(key, shape, pieces, -0.22, 0.18)
    return jnp.clip(array, -bound, bound).astype(kind)


def setup_inputs(seed: int = 0) -> dict:
    streams_of = jax.random.split(jax.random.key(seed), 9)
    hidden_in = bell_draw(streams_of[0], (TOKENS, D), 1.0, 6.0, ((0, 16), (1, 16)))
    grad_gate = bell_draw(streams_of[1], (TOKENS, FF), 1.0, 6.0, ((0, 16), (1, 16)))
    adapter_in = bell_draw(streams_of[2], (TEN, ADAPTER_RANK, D), 0.04, 0.23925781, ((0, 16), (2, 16)))
    adapter_out = bell_draw(streams_of[3], (TEN, ADAPTER_RANK, FF), FF ** -0.5, 0.046875, ((0, 16), (2, 16)))
    block_tenant = touch_ends(ranked(streams_of[4], (NBLK,), TEN, 2), jax.random.fold_in(streams_of[4], 3), 0, TEN - 1).astype(jnp.int32)
    block_dest_keys = jax.random.split(jax.random.fold_in(streams_of[5], 1), NBLK // BLK_G)
    block_dest_turns = jax.random.permutation(jax.random.fold_in(streams_of[5], 3), NBLK // BLK_G)
    block_dest = jax.vmap(lambda own, number: deal_out(jax.random.fold_in(streams_of[5], 2), own, number, BLK_G, N_DP, 1, SEND, 2))(block_dest_keys, block_dest_turns).reshape((NBLK, 1))
    tenant_tokens = touch_ends(jax.random.randint(streams_of[6], (TEN,), 128, 1025), jax.random.fold_in(streams_of[6], 1), 128, 1024).astype(jnp.int32)
    tenant_owner = jax.random.permutation(streams_of[7], TEN).astype(jnp.int32)
    return {"hidden_in": hidden_in, "grad_gate": grad_gate, "adapter_in": adapter_in, "adapter_out": adapter_out, "block_tenant": block_tenant, "block_dest": block_dest, "tenant_tokens": tenant_tokens, "tenant_owner": tenant_owner}


adapter_scale = 2.0

def slot_of_blocks(block_dest):
    target = block_dest[:, 0]
    matches = (target[:, None] == jnp.arange(N_DP, dtype=jnp.int32)[None, :]).astype(jnp.int32)
    matches = matches.reshape(N_DP, BLK_G, N_DP)
    within = lax.optimization_barrier(jnp.sum((jnp.cumsum(matches, axis=1) - matches) * matches, axis=2)).reshape(NBLK)
    source = jnp.arange(NBLK, dtype=jnp.int32) // BLK_G
    return target * SLOTS + source * SEND + within

def reference(hidden_in, grad_gate, adapter_in, adapter_out, block_tenant, block_dest, tenant_tokens, tenant_owner):
    global_slot = slot_of_blocks(block_dest).astype(jnp.int32)
    position = tenant_owner[block_tenant].astype(jnp.int32)
    weight_matrices = 1.0 / tenant_tokens[block_tenant].astype(jnp.float32)
    zero_in = jnp.zeros((TEN, ADAPTER_RANK, D), jnp.float32)
    zero_out = jnp.zeros((TEN, ADAPTER_RANK, FF), jnp.float32)

    def one_block(running, block_index):
        grads_in, grads_out = running
        row_start = (block_index * PLAN_BLOCK_ROWS).astype(jnp.int32)
        rows_x = lax.dynamic_slice_in_dim(hidden_in, row_start, PLAN_BLOCK_ROWS, 0)
        gradient_rows = lax.dynamic_slice_in_dim(grad_gate, row_start, PLAN_BLOCK_ROWS, 0)
        owner_row = position[block_index]
        mat_in = adapter_in[owner_row]
        output_matrix = adapter_out[owner_row]
        rank_product = jnp.dot(rows_x, mat_in.T, preferred_element_type=jnp.float32).astype(jnp.bfloat16)
        rank_matrix = (adapter_scale * jnp.dot(gradient_rows, output_matrix.T, preferred_element_type=jnp.float32)).astype(jnp.bfloat16)
        dgrad_rows = jnp.dot(rank_matrix, mat_in, preferred_element_type=jnp.float32).astype(jnp.bfloat16)
        current_scale = weight_matrices[block_index]
        part_in = jnp.dot(rank_matrix.T, rows_x, preferred_element_type=jnp.float32) * current_scale
        partial_output = jnp.dot(rank_product.T, gradient_rows, preferred_element_type=jnp.float32) * (adapter_scale * current_scale)
        grads_in = grads_in.at[owner_row].add(part_in)
        grads_out = grads_out.at[owner_row].add(partial_output)
        return ((grads_in, grads_out), dgrad_rows)
    (grads_in, grads_out), dgrads = lax.scan(one_block, (zero_in, zero_out), jnp.arange(NBLK, dtype=jnp.int32))
    placed = jnp.zeros((N_DP * SLOTS, PLAN_BLOCK_ROWS, D), jnp.bfloat16).at[global_slot].set(dgrads)
    tenant_norms = jnp.sqrt(lax.optimization_barrier(jnp.sum(grads_in * grads_in, axis=(1, 2))) + lax.optimization_barrier(jnp.sum(grads_out * grads_out, axis=(1, 2))))
    return (placed.reshape(N_DP * SLOTS * PLAN_BLOCK_ROWS, D), grads_in, grads_out, tenant_norms)
```

```python
import functools

import jax
import jax.numpy as jnp
from jax import lax
from jax.experimental import pallas as pl
from jax.experimental.pallas import tpu as pltpu
from jax.sharding import PartitionSpec as P

SIDE = 4
R = 16
ROWS = 128
BLK = 16
OWN = 4
GROUPS = SIDE * SIDE
MESH = pl.DeviceIdType.MESH
BF16 = jnp.bfloat16
F32 = jnp.float32


def remote(src, dst, send_sem, recv_sem, device):
    return pltpu.make_async_remote_copy(
        src_ref=src,
        dst_ref=dst,
        send_sem=send_sem,
        recv_sem=recv_sem,
        device_id=device,
        device_id_type=MESH,
    )


class Ring:
    def __init__(self, buf, here, right, left, sends, recvs, src=None):
        self.buf, self.here, self.right, self.left = buf, here, right, left
        half = buf.shape[1] // 2
        before, after = (here + 3) % SIDE, (here + 1) % SIDE
        own = buf.at[here] if src is None else src
        mine = buf.at[here]
        self.own = [
            remote(own, mine, sends.at[0], recvs.at[0], right),
            remote(own, mine, sends.at[1], recvs.at[1], left),
        ]
        low = buf.at[before, pl.ds(0, half)]
        high = buf.at[after, pl.ds(half, half)]
        self.pass_on = [
            remote(low, low, sends.at[2], recvs.at[2], right),
            remote(high, high, sends.at[3], recvs.at[3], left),
        ]

    def start(self):
        for copy in self.own:
            copy.start()

    def forward(self):
        for copy, onward in zip(self.own, self.pass_on):
            copy.wait_recv()
            onward.start()

    def finish(self):
        for copy in self.pass_on:
            copy.wait_recv()

    def drain(self):
        for copy in self.own + self.pass_on:
            copy.wait_send()


def kernel(
    n_tensor,
    tenant_ref,
    dest_ref,
    tokens_ref,
    owner_ref,
    x_hbm,
    g_hbm,
    ain_hbm,
    aout_hbm,
    dg_hbm,
    gin_hbm,
    gout_hbm,
    norm_ref,
    x_v,
    g_v,
    tab_in,
    tab_out,
    low_part,
    fac_part,
    low_got,
    fac_got,
    low_all,
    fac_all,
    term_in,
    term_out,
    pick,
    sum_in,
    sum_out,
    to_in,
    to_out,
    from_in,
    from_out,
    slot_send,
    slots,
    dg_v,
    gin_v,
    gout_v,
    sq_own,
    sq_got,
    pos_own,
    pos_slot,
    ring_s,
    ring_r,
    z_s,
    z_r,
    slot_s,
    slot_r,
    own_s,
    own_r,
    sq_s,
    sq_r,
    loc,
    dg_sem,
):
    me = lax.axis_index("dp")
    t = lax.axis_index("tensor")
    y, x = me // SIDE, me % SIDE
    bt = BLK // n_tensor
    cd, cf = x_v.shape[1], g_v.shape[1]
    hd, hf = cd // 2, cf // 2

    def at_dp(yy, xx):
        return {"dp": yy * SIDE + xx}

    x_right, x_left = at_dp(y, (x + 1) % SIDE), at_dp(y, (x + 3) % SIDE)
    y_right, y_left = at_dp((y + 1) % SIDE, x), at_dp((y + 3) % SIDE, x)
    along_x, along_y = (x, x_right, x_left), (y, y_right, y_left)

    load_x = pltpu.make_async_copy(x_hbm, x_v, loc.at[0])
    load_g = pltpu.make_async_copy(g_hbm, g_v, loc.at[1])
    in_cols = [ain_hbm.at[:, :, pl.ds(h * hd, hd)] for h in range(2)]
    out_cols = [aout_hbm.at[:, :, pl.ds(h * hf, hf)] for h in range(2)]
    places = [(y, x), (x, y)]
    own_tables = []
    for h in range(2):
        own_tables.append(
            pltpu.make_async_copy(in_cols[h], tab_in[h].at[places[h][0], places[h][1]], loc.at[2 + h])
        )
        own_tables.append(
            pltpu.make_async_copy(
                out_cols[h], tab_out[h].at[places[h][0], places[h][1]], loc.at[4 + h]
            )
        )
    for copy in own_tables:
        copy.start()
    load_x.start()
    load_g.start()

    barrier = pltpu.get_barrier_semaphore()

    def greet_dp(k, _):
        pl.semaphore_signal(
            barrier, inc=1, device_id={"dp": (me + k) % GROUPS}, device_id_type=MESH
        )
        return 0

    def greet_tensor(k, _):
        pl.semaphore_signal(
            barrier, inc=1, device_id={"tensor": (t + k) % n_tensor}, device_id_type=MESH
        )
        return 0

    lax.fori_loop(1, GROUPS, greet_dp, 0)
    lax.fori_loop(1, n_tensor, greet_tensor, 0)

    def place_of(block):
        return owner_ref[tenant_ref[block]]

    def own_places(b, _):
        pos_own[b] = place_of(me * BLK + b)
        return 0

    lax.fori_loop(0, BLK, own_places, 0)
    pl.semaphore_wait(barrier, GROUPS - 1 + n_tensor - 1)

    def ring(number, buf, along, src=None):
        return Ring(buf, along[0], along[1], along[2], ring_s.at[number], ring_r.at[number], src)

    first, second = [along_x, along_y], [along_y, along_x]
    in_1 = [ring(h, tab_in[h].at[places[h][0]], first[h], in_cols[h]) for h in range(2)]
    in_2 = [ring(2 + h, tab_in[h], second[h]) for h in range(2)]
    out_1 = [ring(4 + h, tab_out[h].at[places[h][0]], first[h], out_cols[h]) for h in range(2)]
    out_2 = [ring(6 + h, tab_out[h], second[h]) for h in range(2)]
    for r in in_1 + out_1:
        r.start()
    for copy in own_tables:
        copy.wait()
    for r in in_1 + out_1:
        r.forward()
    for r, after in zip(in_1 + out_1, in_2 + out_2):
        r.finish()
        after.start()

    def slot_places(s, _):
        one, two = jnp.int32(-1), jnp.int32(-1)
        for i in range(BLK):
            b = s * BLK + i
            hit = dest_ref[b] == me
            p = place_of(b)
            two = jnp.where(hit & (one >= 0), p, two)
            one = jnp.where(hit & (one < 0), p, one)
        pos_slot[2 * s] = jnp.maximum(one, 0)
        pos_slot[2 * s + 1] = jnp.maximum(two, 0)
        return 0

    lax.fori_loop(0, GROUPS, slot_places, 0)

    def choose(q, _):
        lane = lax.broadcasted_iota(jnp.int32, (8, 128), 1)
        wide = (SIDE * OWN * R, 128)
        row = lax.broadcasted_iota(jnp.int32, wide, 0)
        same = (row & (R - 1)) == (lax.broadcasted_iota(jnp.int32, wide, 1) & (R - 1))
        tall = row >> 4
        g, first_blk = q // 2, (q % 2) * 8
        for h in range(2):
            group = y * SIDE + g if h == 0 else g * SIDE + x
            want = jnp.full((8, 128), -1, jnp.int32)
            for i in range(8):
                p = place_of(group * BLK + first_blk + i)
                if h == 0:
                    local = jnp.where(((p >> 2) & 3) == x, ((p >> 4) << 2) | (p & 3), -1)
                else:
                    local = jnp.where((p >> 4) == y, p & 15, -1)
                want = jnp.where((lane >> 4) == i, local, want)
            hit = (tall == want[0:1]) & same
            pick[h][:, pl.ds(pl.multiple_of(q * 128, 128), 128)] = jnp.where(hit, 1.0, 0.0).astype(BF16)
        return 0

    lax.fori_loop(0, 2 * SIDE, choose, 0)

    def partial_products(table, rows_v, half, part):
        def one(b, _):
            p = pos_own[b]
            rows = rows_v[pl.ds(pl.multiple_of(b * ROWS, ROWS), ROWS), :]
            tab_a = table[0][p >> 4, (p >> 2) & 3, p & 3]
            tab_b = table[1][(p >> 2) & 3, p >> 4, p & 3]
            nt = (((1,), (1,)), ((), ()))
            part[b] = lax.dot_general(
                tab_a, rows[:, :half], nt, preferred_element_type=F32
            ) + lax.dot_general(tab_b, rows[:, half:], nt, preferred_element_type=F32)
            return 0

        lax.fori_loop(0, BLK, one, 0, unroll=2)

    def reduce_copy(part, got, number, k):
        to = (t + k) % n_tensor
        return remote(
            part.at[pl.ds(to * bt, bt)],
            got.at[k],
            z_s.at[number, k],
            z_r.at[number, k],
            {"tensor": to},
        )

    def spread_copy(full, number, k):
        mine = full.at[pl.ds(t * bt, bt)]
        return remote(
            mine, mine, z_s.at[number, k], z_r.at[number, k], {"tensor": (t + k) % n_tensor}
        )

    def over_tensor(do):
        lax.fori_loop(1, n_tensor, lambda k, _: (do(k), 0)[1], 0)

    def send_parts(part, got, number):
        over_tensor(lambda k: reduce_copy(part, got, number, k).start())

    def add_parts(part, got, full, number, scale):
        over_tensor(lambda k: reduce_copy(part, got, number, k).wait_recv())
        total = lax.fori_loop(1, n_tensor, lambda k, acc: acc + got[k], part[pl.ds(t * bt, bt)])
        full[pl.ds(t * bt, bt)] = (scale * total).astype(BF16)
        over_tensor(lambda k: spread_copy(full, number + 1, k).start())

    def take_spread(full, number):
        over_tensor(lambda k: spread_copy(full, number, k).wait_recv())

    def terms(factor, rows_v, half, out):
        for h in range(2):

            def one(b, _):
                rows = rows_v[pl.ds(pl.multiple_of(b * ROWS, ROWS), ROWS), pl.ds(h * half, half)]
                out[h][first[h][0], b] = jnp.dot(
                    factor[b], rows, preferred_element_type=F32
                ).astype(BF16)
                return 0

            lax.fori_loop(0, BLK, one, 0, unroll=2)

    for r in in_2:
        r.forward()
    for r in in_2:
        r.finish()
    load_x.wait()
    partial_products(tab_in, x_v, hd, low_part)
    send_parts(low_part, low_got, 0)
    for r in out_2:
        r.forward()
    add_parts(low_part, low_got, low_all, 0, 1.0)
    load_g.wait()
    take_spread(low_all, 1)
    term_out_1 = [ring(8 + h, term_out[h], first[h]) for h in range(2)]
    terms(low_all, g_v, hf, term_out)
    for r in term_out_1:
        r.start()
    for r in out_2:
        r.finish()
    partial_products(tab_out, g_v, hf, fac_part)
    send_parts(fac_part, fac_got, 2)
    for r in term_out_1:
        r.forward()
    add_parts(fac_part, fac_got, fac_all, 2, 2.0)
    take_spread(fac_all, 3)
    term_in_1 = [ring(10 + h, term_in[h], first[h]) for h in range(2)]
    terms(fac_all, x_v, hd, term_in)
    for r in term_in_1:
        r.start()

    def slot_copy(k):
        to = (me + k) % GROUPS
        return remote(slot_send.at[k], slots.at[me], slot_s.at[k], slot_r.at[k], {"dp": to})

    def blocks_for(group):
        one, two = jnp.int32(-1), jnp.int32(-1)
        for i in range(BLK):
            hit = dest_ref[me * BLK + i] == group
            two = jnp.where(hit & (one >= 0), i, two)
            one = jnp.where(hit & (one < 0), i, one)
        return one, two

    def masked(i):
        live = jnp.where(i >= 0, 1.0, 0.0).astype(F32)
        return (fac_all[jnp.maximum(i, 0)].astype(F32) * live).astype(BF16)

    def pack(k, _):
        one, two = blocks_for((me + k) % GROUPS)
        slot_send[k, 0] = masked(one)
        slot_send[k, 1] = masked(two)
        slot_copy(k).start()
        return 0

    lax.fori_loop(1, GROUPS, pack, 0)
    one, two = blocks_for(me)
    slots[me, 0] = masked(one)
    slots[me, 1] = masked(two)

    def owner_copies(number, h, sends, lands):
        here = second[h][0]
        copies = []
        for k in range(1, SIDE):
            to = (here + k) % SIDE
            device = at_dp(to, x) if h == 0 else at_dp(y, to)
            copies.append(
                remote(
                    sends.at[to],
                    lands.at[k - 1],
                    own_s.at[number, k - 1],
                    own_r.at[number, k - 1],
                    device,
                )
            )
        return copies

    def add_terms(h, term, total, sends):
        cols = total.shape[1]
        step = min(cols, 256)
        rows = SIDE * OWN * R

        def one(c, _):
            where = pl.ds(pl.multiple_of(c * step, step), step)
            block = term[:, :, :, where].reshape(SIDE * BLK * R, step)
            out = jnp.dot(pick[h][...], block, preferred_element_type=F32)
            total[:, where] = out
            sends[:, :, where] = out.reshape(SIDE, OWN * R, step).astype(BF16)
            return 0

        lax.fori_loop(0, cols // step, one, 0)

    def own_sum(h, total, lands, result, scale, half):
        here = second[h][0]
        kept = total[pl.ds(pl.multiple_of(here * OWN * R, OWN * R), OWN * R), :]
        for k in range(SIDE - 1):
            kept = kept + lands[k].astype(F32)
        squares = []
        for j in range(OWN):
            piece = kept[j * R : (j + 1) * R] * scale[j]
            result[j, :, pl.ds(h * half, half)] = piece
            squares.append(jnp.sum(piece * piece, axis=0, keepdims=True))
        return squares

    out_own = [owner_copies(h, h, to_out[h], from_out[h]) for h in range(2)]
    in_own = [owner_copies(2 + h, h, to_in[h], from_in[h]) for h in range(2)]
    for h in range(2):
        term_out_1[h].finish()
        add_terms(h, term_out[h], sum_out[h], to_out[h])
        for copy in out_own[h]:
            copy.start()
    for r in term_in_1:
        r.forward()

    def await_slots(k, _):
        slot_copy(k).wait_recv()
        return 0

    lax.fori_loop(1, GROUPS, await_slots, 0)

    def dg_copy(s):
        rows = pl.ds(pl.multiple_of(s * 2 * ROWS, 2 * ROWS), 2 * ROWS)
        return pltpu.make_async_copy(dg_v.at[rows], dg_hbm.at[rows], dg_sem.at[s])

    def apply_factor(s, _):
        tn = (((0,), (0,)), ((), ()))
        for w in range(2):
            p = pos_slot[2 * s + w]
            factor = slots[s, w]
            rows = pl.ds(pl.multiple_of((2 * s + w) * ROWS, ROWS), ROWS)
            dg_v[rows, :hd] = lax.dot_general(
                factor, tab_in[0][p >> 4, (p >> 2) & 3, p & 3], tn, preferred_element_type=F32
            ).astype(BF16)
            dg_v[rows, hd:] = lax.dot_general(
                factor, tab_in[1][(p >> 2) & 3, p >> 4, p & 3], tn, preferred_element_type=F32
            ).astype(BF16)
        dg_copy(s).start()
        return 0

    lax.fori_loop(0, GROUPS, apply_factor, 0)

    for h in range(2):
        term_in_1[h].finish()
        add_terms(h, term_in[h], sum_in[h], to_in[h])
        for copy in in_own[h]:
            copy.start()

    def find(k, found):
        at = owner_ref[k] - me * OWN
        return tuple(jnp.where(at == j, tokens_ref[k], found[j]) for j in range(OWN))

    found = lax.fori_loop(0, owner_ref.shape[0], find, (jnp.int32(1),) * OWN)
    weight = [1.0 / jnp.full((1, 128), f, jnp.int32).astype(F32) for f in found]

    def weigh(half, by):
        return [jnp.tile(by * w, (1, half // 128)) for w in weight]

    for h in range(2):
        for copy in out_own[h]:
            copy.wait_recv()
    parts = [own_sum(h, sum_out[h], from_out[h], gout_v, weigh(hf, 2.0), hf) for h in range(2)]
    save_out = pltpu.make_async_copy(gout_v, gout_hbm, loc.at[6])
    save_out.start()
    for h in range(2):
        for copy in in_own[h]:
            copy.wait_recv()
    parts += [own_sum(h, sum_in[h], from_in[h], gin_v, weigh(hd, 1.0), hd) for h in range(2)]
    save_in = pltpu.make_async_copy(gin_v, gin_hbm, loc.at[7])
    save_in.start()

    row8 = lax.broadcasted_iota(jnp.int32, (8, 128), 0)
    square = jnp.zeros((8, 128), F32)
    for j in range(OWN):
        one_sum = jnp.zeros((1, 128), F32)
        for part in parts:
            for c in range(part[j].shape[1] // 128):
                one_sum = one_sum + part[j][:, c * 128 : (c + 1) * 128]
        square = jnp.where(row8 == j, one_sum, square)
    sq_own[...] = square

    def square_copy(k):
        return remote(
            sq_own, sq_got.at[k], sq_s.at[k], sq_r.at[k], {"tensor": (t + k) % n_tensor}
        )

    over_tensor(lambda k: square_copy(k).start())
    over_tensor(lambda k: square_copy(k).wait_recv())
    total = lax.fori_loop(1, n_tensor, lambda k, acc: acc + sq_got[k], sq_own[...])
    norm_ref[...] = jnp.sqrt(jnp.broadcast_to(jnp.sum(total, axis=1, keepdims=True), (8, 128)))

    for r in in_1 + in_2 + out_1 + out_2 + term_out_1 + term_in_1:
        r.drain()
    for copies in out_own + in_own:
        for copy in copies:
            copy.wait_send()
    over_tensor(lambda k: reduce_copy(low_part, low_got, 0, k).wait_send())
    over_tensor(lambda k: spread_copy(low_all, 1, k).wait_send())
    over_tensor(lambda k: reduce_copy(fac_part, fac_got, 2, k).wait_send())
    over_tensor(lambda k: spread_copy(fac_all, 3, k).wait_send())
    over_tensor(lambda k: square_copy(k).wait_send())

    def drain_slots(k, _):
        slot_copy(k).wait_send()
        return 0

    lax.fori_loop(1, GROUPS, drain_slots, 0)

    def drain_dg(s, _):
        dg_copy(s).wait()
        return 0

    lax.fori_loop(0, GROUPS, drain_dg, 0)
    save_out.wait()
    save_in.wait()


def per_device(
    hidden_in, grad_gate, adapter_in, adapter_out, block_tenant, block_dest, tenant_tokens, tenant_owner
):
    n_tensor = lax.axis_size("tensor")
    bt = BLK // n_tensor
    cd, cf = hidden_in.shape[1], grad_gate.shape[1]
    hd, hf = cd // 2, cf // 2
    wide = SIDE * OWN * R

    def pair(shape, dtype):
        return [pltpu.VMEM(shape, dtype), pltpu.VMEM(shape, dtype)]

    dma = pltpu.SemaphoreType.DMA
    smem = pl.BlockSpec(memory_space=pltpu.SMEM)
    hbm = pl.BlockSpec(memory_space=pltpu.HBM)
    scratch = [
        pltpu.VMEM(hidden_in.shape, BF16),
        pltpu.VMEM(grad_gate.shape, BF16),
        pair((SIDE, SIDE, OWN, R, hd), BF16),
        pair((SIDE, SIDE, OWN, R, hf), BF16),
        pltpu.VMEM((BLK, R, ROWS), F32),
        pltpu.VMEM((BLK, R, ROWS), F32),
        pltpu.VMEM((n_tensor, bt, R, ROWS), F32),
        pltpu.VMEM((n_tensor, bt, R, ROWS), F32),
        pltpu.VMEM((BLK, R, ROWS), BF16),
        pltpu.VMEM((BLK, R, ROWS), BF16),
        pair((SIDE, BLK, R, hd), BF16),
        pair((SIDE, BLK, R, hf), BF16),
        pair((wide, SIDE * BLK * R), BF16),
        pair((wide, hd), F32),
        pair((wide, hf), F32),
        pair((SIDE, OWN * R, hd), BF16),
        pair((SIDE, OWN * R, hf), BF16),
        pair((SIDE - 1, OWN * R, hd), BF16),
        pair((SIDE - 1, OWN * R, hf), BF16),
        pltpu.VMEM((GROUPS, 2, R, ROWS), BF16),
        pltpu.VMEM((GROUPS, 2, R, ROWS), BF16),
        pltpu.VMEM((GROUPS * 2 * ROWS, cd), BF16),
        pltpu.VMEM((OWN, R, cd), F32),
        pltpu.VMEM((OWN, R, cf), F32),
        pltpu.VMEM((8, 128), F32),
        pltpu.VMEM((n_tensor, 8, 128), F32),
        pltpu.SMEM((BLK,), jnp.int32),
        pltpu.SMEM((2 * GROUPS,), jnp.int32),
        dma((12, 4)),
        dma((12, 4)),
        dma((4, n_tensor)),
        dma((4, n_tensor)),
        dma((GROUPS,)),
        dma((GROUPS,)),
        dma((4, SIDE - 1)),
        dma((4, SIDE - 1)),
        dma((n_tensor,)),
        dma((n_tensor,)),
        dma((8,)),
        dma((GROUPS,)),
    ]
    dgrad, grad_in, grad_out, norms = pl.pallas_call(
        functools.partial(kernel, n_tensor),
        out_shape=(
            jax.ShapeDtypeStruct((GROUPS * 2 * ROWS, cd), BF16),
            jax.ShapeDtypeStruct((OWN, R, cd), F32),
            jax.ShapeDtypeStruct((OWN, R, cf), F32),
            jax.ShapeDtypeStruct((8, 128), F32),
        ),
        in_specs=[smem] * 4 + [hbm] * 4,
        out_specs=(hbm, hbm, hbm, pl.BlockSpec(memory_space=pltpu.VMEM)),
        scratch_shapes=scratch,
        compiler_params=pltpu.CompilerParams(
            collective_id=0, has_side_effects=True, vmem_limit_bytes=60 * 1024 * 1024
        ),
    )(
        block_tenant,
        block_dest.reshape(-1),
        tenant_tokens,
        tenant_owner,
        hidden_in,
        grad_gate,
        adapter_in,
        adapter_out,
    )
    return dgrad, grad_in, grad_out, norms[:OWN, 0]


def solution(mesh):
    return jax.shard_map(
        per_device,
        mesh=mesh,
        in_specs=(
            P("dp", "tensor"),
            P("dp", "tensor"),
            P("dp", None, "tensor"),
            P("dp", None, "tensor"),
            P(),
            P(),
            P(),
            P(),
        ),
        out_specs=(P("dp", "tensor"), P("dp", None, "tensor"), P("dp", None, "tensor"), P("dp")),
        check_vma=False,
    )
```

```python
import functools

import jax
import jax.numpy as jnp
from jax import lax
from jax.experimental import pallas as pl
from jax.experimental.pallas import tpu as pltpu
from jax.sharding import PartitionSpec as P

SIDE = 4
R = 16
ROWS = 128
BLK = 16
OWN = 4
GROUPS = SIDE * SIDE
MESH = pl.DeviceIdType.MESH
BF16 = jnp.bfloat16
F32 = jnp.float32


def remote(src, dst, send_sem, recv_sem, device):
    return pltpu.make_async_remote_copy(
        src_ref=src,
        dst_ref=dst,
        send_sem=send_sem,
        recv_sem=recv_sem,
        device_id=device,
        device_id_type=MESH,
    )


def await_bytes(ref, sem):
    pltpu.make_async_copy(ref, ref, sem).wait()


class Gather:
    def __init__(self, buf, first, second, ring, number, src):
        a, b = first[0], second[0]
        column = [buf.at[:, (a + k) % SIDE] for k in (0, 3, 1, 2)]
        row = ring(number, buf.at[b], first, src, True)
        mine = ring(number + 1, column[0], second, src, False)
        before, after, far = [ring(number + 1 + k, column[k], second, None, False) for k in (1, 2, 3)]

        def come(way, onward):
            def step():
                row.forward_one(way)
                onward.start()

            return step

        def opposite():
            row.finish()
            far.start()

        self.steps = [
            [row.start, mine.start],
            [come(0, before), come(1, after), opposite, mine.forward],
            [before.forward, after.forward],
            [far.forward, mine.finish],
            [before.finish, after.finish, far.finish],
        ]
        self.rings = (row, mine, before, after, far)

    def drain(self):
        for r in self.rings:
            r.drain()


class Ring:
    def __init__(self, buf, here, right, left, far, sends, recvs, src=None, direct=False):
        self.buf, self.here, self.right, self.left = buf, here, right, left
        half = buf.shape[1] // 2
        before, after = (here + 3) % SIDE, (here + 1) % SIDE
        own = buf.at[here] if src is None else src
        mine = buf.at[here]
        self.sends, self.recvs = sends, recvs
        self.own = [
            remote(own, mine, sends, recvs.at[0], right),
            remote(own, mine, sends, recvs.at[1], left),
        ]
        low = buf.at[before, pl.ds(0, half)]
        high = buf.at[after, pl.ds(half, half)]
        self.pass_on = [
            remote(low, low, sends, recvs.at[2], right),
            remote(high, high, sends, recvs.at[2], left),
        ]
        self.direct = direct
        if direct:
            self.own.append(remote(own, mine, sends, recvs.at[2], far))

    def start(self):
        for copy in self.own:
            copy.start()

    def forward_one(self, way):
        self.own[way].wait_recv()
        if not self.direct:
            self.pass_on[way].start()

    def forward(self):
        self.forward_one(0)
        self.forward_one(1)

    def finish(self):
        await_bytes(self.buf.at[(self.here + 2) % SIDE], self.recvs.at[2])

    def drain(self):
        await_bytes(self.buf.at[pl.ds(0, SIDE - 1)], self.sends)


def kernel(
    n_tensor,
    tenant_ref,
    dest_ref,
    tokens_ref,
    owner_ref,
    x_hbm,
    g_hbm,
    ain_hbm,
    aout_hbm,
    slots_hbm,
    sel_hbm,
    gin_hbm,
    gout_hbm,
    norm_ref,
    x_v,
    g_v,
    tab_in,
    tab_out,
    low_part,
    fac_part,
    low_got,
    fac_got,
    low_all,
    fac_all,
    term_in,
    term_out,
    pick,
    sum_in,
    sum_out,
    to_in,
    to_out,
    from_in,
    from_out,
    slot_send,
    slots,
    sel_v,
    gin_v,
    gout_v,
    sq_own,
    sq_got,
    pos_own,
    pos_slot,
    ring_s,
    ring_r,
    z_s,
    z_r,
    slot_sem,
    own_s,
    own_r,
    sq_sem,
    loc,
):
    me = lax.axis_index("dp")
    t = lax.axis_index("tensor")
    y, x = me // SIDE, me % SIDE
    bt = BLK // n_tensor
    cd, cf = x_v.shape[1], g_v.shape[1]
    hd, hf = cd // 2, cf // 2

    ends = []

    def at_dp(yy, xx):
        return {"dp": yy * SIDE + xx}

    x_right, x_left = at_dp(y, (x + 1) % SIDE), at_dp(y, (x + 3) % SIDE)
    y_right, y_left = at_dp((y + 1) % SIDE, x), at_dp((y + 3) % SIDE, x)
    x_far, y_far = at_dp(y, (x + 2) % SIDE), at_dp((y + 2) % SIDE, x)
    along_x, along_y = (x, x_right, x_left, x_far), (y, y_right, y_left, y_far)

    load_x = pltpu.make_async_copy(x_hbm, x_v, loc.at[0])
    load_g = pltpu.make_async_copy(g_hbm, g_v, loc.at[1])
    in_cols = [ain_hbm.at[:, :, pl.ds(h * hd, hd)] for h in range(2)]
    out_cols = [aout_hbm.at[:, :, pl.ds(h * hf, hf)] for h in range(2)]
    places = [(y, x), (x, y)]
    own_tables = []
    for h in range(2):
        own_tables.append(
            pltpu.make_async_copy(in_cols[h], tab_in[h].at[places[h][0], places[h][1]], loc.at[2 + h])
        )
        own_tables.append(
            pltpu.make_async_copy(
                out_cols[h], tab_out[h].at[places[h][0], places[h][1]], loc.at[4 + h]
            )
        )
    for copy in own_tables:
        copy.start()
    load_x.start()
    load_g.start()

    barrier = pltpu.get_barrier_semaphore()

    def greet_dp(k, _):
        pl.semaphore_signal(
            barrier, inc=1, device_id={"dp": (me + k) % GROUPS}, device_id_type=MESH
        )
        return 0

    def greet_tensor(k, _):
        pl.semaphore_signal(
            barrier, inc=1, device_id={"tensor": (t + k) % n_tensor}, device_id_type=MESH
        )
        return 0

    lax.fori_loop(1, GROUPS, greet_dp, 0)
    lax.fori_loop(1, n_tensor, greet_tensor, 0)

    def place_of(block):
        return owner_ref[tenant_ref[block]]

    def own_places(b, _):
        pos_own[b] = place_of(me * BLK + b)
        return 0

    lax.fori_loop(0, BLK, own_places, 0)
    pl.semaphore_wait(barrier, GROUPS - 1 + n_tensor - 1)

    def slot_places(s, _):
        one, two = jnp.int32(-1), jnp.int32(-1)
        for i in range(BLK):
            b = s * BLK + i
            hit = dest_ref[b] == me
            p = place_of(b)
            two = jnp.where(hit & (one >= 0), p, two)
            one = jnp.where(hit & (one < 0), p, one)
        pos_slot[2 * s] = jnp.maximum(one, 0)
        pos_slot[2 * s + 1] = jnp.maximum(two, 0)
        return 0

    def slot_tables():
        lax.fori_loop(0, GROUPS, slot_places, 0)

    def choose(q, _):
        lane = lax.broadcasted_iota(jnp.int32, (8, 128), 1)
        wide = (SIDE * OWN * R, 128)
        row = lax.broadcasted_iota(jnp.int32, wide, 0)
        same = (row & (R - 1)) == (lax.broadcasted_iota(jnp.int32, wide, 1) & (R - 1))
        tall = row >> 4
        g, first_blk = q // 2, (q % 2) * 8
        for h in range(2):
            group = y * SIDE + g if h == 0 else g * SIDE + x
            want = jnp.full((8, 128), -1, jnp.int32)
            for i in range(8):
                p = place_of(group * BLK + first_blk + i)
                if h == 0:
                    local = jnp.where(((p >> 2) & 3) == x, ((p >> 4) << 2) | (p & 3), -1)
                else:
                    local = jnp.where((p >> 4) == y, p & 15, -1)
                want = jnp.where((lane >> 4) == i, local, want)
            hit = (tall == want[0:1]) & same
            pick[h][:, pl.ds(pl.multiple_of(q * 128, 128), 128)] = jnp.where(hit, 1.0, 0.0).astype(BF16)
        return 0

    def choose_all():
        lax.fori_loop(0, 2 * SIDE, choose, 0)

    def find(k, found):
        at = owner_ref[k] - me * OWN
        return tuple(jnp.where(at == j, tokens_ref[k], found[j]) for j in range(OWN))

    def owned_weights():
        found = lax.fori_loop(0, owner_ref.shape[0], find, (jnp.int32(1),) * OWN)
        return [1.0 / jnp.full((1, 128), f, jnp.int32).astype(F32) for f in found]

    def ring(number, buf, along, src=None, direct=False):
        return Ring(buf, *along, ring_s.at[number], ring_r.at[number], src, direct)

    first, second = [along_x, along_y], [along_y, along_x]
    tab_in_ag = [Gather(tab_in[h], first[h], second[h], ring, 5 * h, in_cols[h]) for h in range(2)]
    tab_out_ag = [
        Gather(tab_out[h], first[h], second[h], ring, 10 + 5 * h, out_cols[h]) for h in range(2)
    ]

    def deep(gathers, depth):
        for part in range(len(gathers[0].steps[depth])):
            for gather in gathers:
                gather.steps[depth][part]()

    for gathers in (tab_in_ag, tab_out_ag):
        deep(gathers, 0)
        ends.extend(g.drain for g in gathers)
    slot_tables()
    for copy in own_tables:
        copy.wait()
    def partial_products(table, rows_v, half, part):
        def one(b, _):
            p = pos_own[b]
            rows = rows_v[pl.ds(pl.multiple_of(b * ROWS, ROWS), ROWS), :]
            tab_a = table[0][p >> 4, (p >> 2) & 3, p & 3]
            tab_b = table[1][(p >> 2) & 3, p >> 4, p & 3]
            nt = (((1,), (1,)), ((), ()))
            part[b] = lax.dot_general(
                tab_a, rows[:, :half], nt, preferred_element_type=F32
            ) + lax.dot_general(tab_b, rows[:, half:], nt, preferred_element_type=F32)
            return 0

        lax.fori_loop(0, BLK, one, 0, unroll=2)

    def reduce_copy(part, got, number, k):
        to = (t + k) % n_tensor
        return remote(
            part.at[pl.ds(to * bt, bt)],
            got.at[k],
            z_s.at[number],
            z_r.at[number],
            {"tensor": to},
        )

    def spread_copy(full, number, k):
        mine = full.at[pl.ds(t * bt, bt)]
        return remote(
            mine, mine, z_s.at[number], z_r.at[number], {"tensor": (t + k) % n_tensor}
        )

    def over_tensor(do):
        lax.fori_loop(1, n_tensor, lambda k, _: (do(k), 0)[1], 0)

    def send_parts(part, got, number):
        over_tensor(lambda k: reduce_copy(part, got, number, k).start())
        ends.append(lambda: await_bytes(got.at[pl.ds(1, n_tensor - 1)], z_s.at[number]))

    def add_parts(part, got, full, number, scale):
        await_bytes(got.at[pl.ds(1, n_tensor - 1)], z_r.at[number])
        total = lax.fori_loop(1, n_tensor, lambda k, acc: acc + got[k], part[pl.ds(t * bt, bt)])
        full[pl.ds(t * bt, bt)] = (scale * total).astype(BF16)
        over_tensor(lambda k: spread_copy(full, number + 1, k).start())
        ends.append(lambda: await_bytes(full.at[pl.ds(0, BLK - bt)], z_s.at[number + 1]))

    def take_spread(full, number):
        await_bytes(full.at[pl.ds(0, BLK - bt)], z_r.at[number])

    def terms(h, factor, rows_v, half, out):
        def one(b, _):
            rows = rows_v[pl.ds(pl.multiple_of(b * ROWS, ROWS), ROWS), pl.ds(h * half, half)]
            out[h][first[h][0], b] = jnp.dot(
                factor[b], rows, preferred_element_type=F32
            ).astype(BF16)
            return 0

        lax.fori_loop(0, BLK, one, 0, unroll=2)

    def select(i, _):
        p = pos_slot[i]
        sel_v[i, :, :hd] = tab_in[0][p >> 4, (p >> 2) & 3, p & 3]
        sel_v[i, :, hd:] = tab_in[1][(p >> 2) & 3, p >> 4, p & 3]
        return 0

    def select_all():
        lax.fori_loop(0, 2 * GROUPS, select, 0, unroll=4)
        save_sel = pltpu.make_async_copy(sel_v, sel_hbm, loc.at[0])
        save_sel.start()
        ends.append(save_sel.wait)

    deep(tab_in_ag, 1)
    deep(tab_out_ag, 1)
    deep(tab_in_ag, 2)
    deep(tab_in_ag, 3)
    deep(tab_out_ag, 2)
    deep(tab_in_ag, 4)
    load_x.wait()
    partial_products(tab_in, x_v, hd, low_part)
    send_parts(low_part, low_got, 0)
    select_all()
    deep(tab_out_ag, 3)
    choose_all()
    add_parts(low_part, low_got, low_all, 0, 1.0)
    load_g.wait()
    deep(tab_out_ag, 4)
    partial_products(tab_out, g_v, hf, fac_part)
    send_parts(fac_part, fac_got, 2)
    take_spread(low_all, 1)
    term_out_1 = [ring(20 + h, term_out[h], first[h], None, False) for h in range(2)]
    for h in range(2):
        terms(h, low_all, g_v, hf, term_out)
        term_out_1[h].start()
        ends.append(term_out_1[h].drain)
    add_parts(fac_part, fac_got, fac_all, 2, 2.0)
    for r in term_out_1:
        r.forward()
    weight = owned_weights()
    take_spread(fac_all, 3)
    term_in_1 = [ring(22 + h, term_in[h], first[h], None, False) for h in range(2)]
    for h in range(2):
        terms(h, fac_all, x_v, hd, term_in)
        term_in_1[h].start()
        ends.append(term_in_1[h].drain)

    def slot_copy(k):
        to = (me + k) % GROUPS
        return remote(slot_send.at[k], slots.at[me], slot_sem.at[0], slot_sem.at[1], {"dp": to})

    def blocks_for(group):
        one, two = jnp.int32(-1), jnp.int32(-1)
        for i in range(BLK):
            hit = dest_ref[me * BLK + i] == group
            two = jnp.where(hit & (one >= 0), i, two)
            one = jnp.where(hit & (one < 0), i, one)
        return one, two

    def masked(i):
        live = jnp.where(i >= 0, 1.0, 0.0).astype(F32)
        return (fac_all[jnp.maximum(i, 0)].astype(F32) * live).astype(BF16)

    def pack(k, _):
        one, two = blocks_for((me + k) % GROUPS)
        slot_send[k, 0] = masked(one)
        slot_send[k, 1] = masked(two)
        slot_copy(k).start()
        return 0

    lax.fori_loop(1, GROUPS, pack, 0)

    ends.append(lambda: await_bytes(slots.at[pl.ds(0, GROUPS - 1)], slot_sem.at[0]))
    one, two = blocks_for(me)
    slots[me, 0] = masked(one)
    slots[me, 1] = masked(two)

    def owner_copies(number, h, sends, lands):
        here = second[h][0]
        copies = []
        for k in range(1, SIDE):
            to = (here + k) % SIDE
            device = at_dp(to, x) if h == 0 else at_dp(y, to)
            copies.append(
                remote(
                    sends.at[to],
                    lands.at[k - 1],
                    own_s.at[number],
                    own_r.at[number],
                    device,
                )
            )
        return copies

    def add_terms(h, term, total, sends):
        cols = total.shape[1]
        step = min(cols, 256)
        rows = SIDE * OWN * R

        def one(c, _):
            where = pl.ds(pl.multiple_of(c * step, step), step)
            block = term[:, :, :, where].reshape(SIDE * BLK * R, step)
            out = jnp.dot(pick[h][...], block, preferred_element_type=F32)
            total[:, where] = out
            sends[:, :, where] = out.reshape(SIDE, OWN * R, step).astype(BF16)
            return 0

        lax.fori_loop(0, cols // step, one, 0)

    def own_sum(h, total, lands, result, scale, half):
        here = second[h][0]
        kept = total[pl.ds(pl.multiple_of(here * OWN * R, OWN * R), OWN * R), :]
        for k in range(SIDE - 1):
            kept = kept + lands[k].astype(F32)
        squares = []
        for j in range(OWN):
            piece = kept[j * R : (j + 1) * R] * scale[j]
            result[j, :, pl.ds(h * half, half)] = piece
            squares.append(jnp.sum(piece * piece, axis=0, keepdims=True))
        return squares

    out_own = [owner_copies(h, h, to_out[h], from_out[h]) for h in range(2)]
    in_own = [owner_copies(2 + h, h, to_in[h], from_in[h]) for h in range(2)]
    for h in range(2):
        term_out_1[h].finish()
        add_terms(h, term_out[h], sum_out[h], to_out[h])
        for copy in out_own[h]:
            copy.start()
    for r in term_in_1:
        r.forward()

    await_bytes(slots.at[pl.ds(0, GROUPS - 1)], slot_sem.at[1])
    save_slots = pltpu.make_async_copy(slots, slots_hbm, loc.at[1])
    save_slots.start()
    ends.append(save_slots.wait)

    for h in range(2):
        term_in_1[h].finish()
        add_terms(h, term_in[h], sum_in[h], to_in[h])
        for copy in in_own[h]:
            copy.start()

    def weigh(half, by):
        return [jnp.tile(by * w, (1, half // 128)) for w in weight]

    for h in range(2):
        await_bytes(from_out[h], own_r.at[h])
    parts = [own_sum(h, sum_out[h], from_out[h], gout_v, weigh(hf, 2.0), hf) for h in range(2)]
    save_out = pltpu.make_async_copy(gout_v, gout_hbm, loc.at[6])
    save_out.start()
    ends.append(save_out.wait)
    for h in range(2):
        await_bytes(from_in[h], own_r.at[2 + h])
    parts += [own_sum(h, sum_in[h], from_in[h], gin_v, weigh(hd, 1.0), hd) for h in range(2)]
    save_in = pltpu.make_async_copy(gin_v, gin_hbm, loc.at[7])
    save_in.start()
    ends.append(save_in.wait)

    for h in range(2):
        ends.append(functools.partial(await_bytes, from_out[h], own_s.at[h]))
        ends.append(functools.partial(await_bytes, from_in[h], own_s.at[2 + h]))

    row8 = lax.broadcasted_iota(jnp.int32, (8, 128), 0)
    square = jnp.zeros((8, 128), F32)
    for j in range(OWN):
        one_sum = jnp.zeros((1, 128), F32)
        for part in parts:
            for c in range(part[j].shape[1] // 128):
                one_sum = one_sum + part[j][:, c * 128 : (c + 1) * 128]
        square = jnp.where(row8 == j, one_sum, square)
    sq_own[...] = square

    def square_copy(k):
        return remote(
            sq_own, sq_got.at[k], sq_sem.at[0], sq_sem.at[1], {"tensor": (t + k) % n_tensor}
        )

    over_tensor(lambda k: square_copy(k).start())
    ends.append(lambda: await_bytes(sq_got.at[pl.ds(1, n_tensor - 1)], sq_sem.at[0]))
    await_bytes(sq_got.at[pl.ds(1, n_tensor - 1)], sq_sem.at[1])
    total = lax.fori_loop(1, n_tensor, lambda k, acc: acc + sq_got[k], sq_own[...])
    norm_ref[...] = jnp.sqrt(jnp.broadcast_to(jnp.sum(total, axis=1, keepdims=True), (8, 128)))

    for end in ends:
        end()


def place(
    slots, sel, gin, gout, norms, dg_to, gin_to, gout_to, norms_to, slots_v, sel_v, dg_v, gin_v, gout_v, sems
):
    cd = dg_v.shape[1]
    quarter = 2 * GROUPS // 4
    load_slots = pltpu.make_async_copy(slots, slots_v, sems.at[0])
    load_slots.start()
    load_sel = []
    for i in range(4):
        some = pl.ds(i * quarter, quarter)
        load_sel.append(pltpu.make_async_copy(sel.at[some], sel_v.at[some], sems.at[1 + i]))
        load_sel[i].start()
    moves = [(gin, gin_v, gin_to), (gout, gout_v, gout_to)]
    loads = [pltpu.make_async_copy(m[0], m[1], sems.at[5 + i]) for i, m in enumerate(moves)]
    saves = [pltpu.make_async_copy(m[1], m[2], sems.at[7 + i]) for i, m in enumerate(moves)]
    for copy in loads:
        copy.start()
    for j in range(OWN):
        norms_to[j] = norms[j, 0]
    load_slots.wait()
    for i in range(4):
        load_sel[i].wait()

        def one(k, _):
            slot = i * quarter + k
            rows = pl.ds(pl.multiple_of(slot * ROWS, ROWS), ROWS)
            dg_v[rows, :] = lax.dot_general(
                slots_v[slot], sel_v[slot], (((0,), (0,)), ((), ())), preferred_element_type=F32
            ).astype(BF16)
            return 0

        lax.fori_loop(0, quarter, one, 0, unroll=4)
        rows = pl.ds(i * quarter * ROWS, quarter * ROWS)
        saves.append(pltpu.make_async_copy(dg_v.at[rows], dg_to.at[rows], sems.at[9 + i]))
        saves[-1].start()
    for load, save in zip(loads, saves):
        load.wait()
        save.start()
    for copy in saves:
        copy.wait()


def per_device(
    hidden_in, grad_gate, adapter_in, adapter_out, block_tenant, block_dest, tenant_tokens, tenant_owner
):
    n_tensor = lax.axis_size("tensor")
    bt = BLK // n_tensor
    cd, cf = hidden_in.shape[1], grad_gate.shape[1]
    hd, hf = cd // 2, cf // 2
    wide = SIDE * OWN * R

    def pair(shape, dtype):
        return [pltpu.VMEM(shape, dtype), pltpu.VMEM(shape, dtype)]

    dma = pltpu.SemaphoreType.DMA
    smem = pl.BlockSpec(memory_space=pltpu.SMEM)
    hbm = pl.BlockSpec(memory_space=pltpu.HBM)
    scratch = [
        pltpu.VMEM(hidden_in.shape, BF16),
        pltpu.VMEM(grad_gate.shape, BF16),
        pair((SIDE, SIDE, OWN, R, hd), BF16),
        pair((SIDE, SIDE, OWN, R, hf), BF16),
        pltpu.VMEM((BLK, R, ROWS), F32),
        pltpu.VMEM((BLK, R, ROWS), F32),
        pltpu.VMEM((n_tensor, bt, R, ROWS), F32),
        pltpu.VMEM((n_tensor, bt, R, ROWS), F32),
        pltpu.VMEM((BLK, R, ROWS), BF16),
        pltpu.VMEM((BLK, R, ROWS), BF16),
        pair((SIDE, BLK, R, hd), BF16),
        pair((SIDE, BLK, R, hf), BF16),
        pair((wide, SIDE * BLK * R), BF16),
        pair((wide, hd), F32),
        pair((wide, hf), F32),
        pair((SIDE, OWN * R, hd), BF16),
        pair((SIDE, OWN * R, hf), BF16),
        pair((SIDE - 1, OWN * R, hd), BF16),
        pair((SIDE - 1, OWN * R, hf), BF16),
        pltpu.VMEM((GROUPS, 2, R, ROWS), BF16),
        pltpu.VMEM((GROUPS, 2, R, ROWS), BF16),
        pltpu.VMEM((2 * GROUPS, R, cd), BF16),
        pltpu.VMEM((OWN, R, cd), F32),
        pltpu.VMEM((OWN, R, cf), F32),
        pltpu.VMEM((8, 128), F32),
        pltpu.VMEM((n_tensor, 8, 128), F32),
        pltpu.SMEM((BLK,), jnp.int32),
        pltpu.SMEM((2 * GROUPS,), jnp.int32),
        dma((24,)),
        dma((24, 3)),
        dma((4,)),
        dma((4,)),
        dma((2,)),
        dma((4,)),
        dma((4,)),
        dma((2,)),
        dma((8,)),
    ]
    results = pl.pallas_call(
        functools.partial(kernel, n_tensor),
        out_shape=(
            jax.ShapeDtypeStruct((GROUPS, 2, R, ROWS), BF16),
            jax.ShapeDtypeStruct((2 * GROUPS, R, cd), BF16),
            jax.ShapeDtypeStruct((OWN, R, cd), F32),
            jax.ShapeDtypeStruct((OWN, R, cf), F32),
            jax.ShapeDtypeStruct((8, 128), F32),
        ),
        in_specs=[smem] * 4 + [hbm] * 4,
        out_specs=(hbm, hbm, hbm, hbm, pl.BlockSpec(memory_space=pltpu.VMEM)),
        scratch_shapes=scratch,
        compiler_params=pltpu.CompilerParams(
            collective_id=0, has_side_effects=True, vmem_limit_bytes=60 * 1024 * 1024
        ),
    )(
        block_tenant,
        block_dest.reshape(-1),
        tenant_tokens,
        tenant_owner,
        hidden_in,
        grad_gate,
        adapter_in,
        adapter_out,
    )
    slots, sel, grad_in, grad_out, norms = results
    return pl.pallas_call(
        place,
        out_shape=(
            jax.ShapeDtypeStruct((GROUPS * 2 * ROWS, cd), BF16),
            jax.ShapeDtypeStruct((OWN, R, cd), F32),
            jax.ShapeDtypeStruct((OWN, R, cf), F32),
            jax.ShapeDtypeStruct((OWN,), F32),
        ),
        in_specs=[hbm] * 4 + [smem],
        out_specs=(hbm, hbm, hbm, smem),
        scratch_shapes=[
            pltpu.VMEM((2 * GROUPS, R, ROWS), BF16),
            pltpu.VMEM((2 * GROUPS, R, cd), BF16),
            pltpu.VMEM((GROUPS * 2 * ROWS, cd), BF16),
            pltpu.VMEM((OWN, R, cd), F32),
            pltpu.VMEM((OWN, R, cf), F32),
            dma((13,)),
        ],
        compiler_params=pltpu.CompilerParams(vmem_limit_bytes=60 * 1024 * 1024),
    )(slots.reshape(2 * GROUPS, R, ROWS), sel, grad_in, grad_out, norms)


def solution(mesh):
    return jax.shard_map(
        per_device,
        mesh=mesh,
        in_specs=(
            P("dp", "tensor"),
            P("dp", "tensor"),
            P("dp", None, "tensor"),
            P("dp", None, "tensor"),
            P(),
            P(),
            P(),
            P(),
        ),
        out_specs=(P("dp", "tensor"), P("dp", None, "tensor"), P("dp", None, "tensor"), P("dp")),
        check_vma=False,
    )
```

```python
import functools

import jax
import jax.numpy as jnp
from jax import lax
from jax.experimental import pallas as pl
from jax.experimental.pallas import tpu as pltpu
from jax.sharding import PartitionSpec as P

SIDE = 4
R = 16
ROWS = 128
BLK = 16
OWN = 4
GROUPS = SIDE * SIDE
MESH = pl.DeviceIdType.MESH
BF16 = jnp.bfloat16
F32 = jnp.float32


def remote(src, dst, send_sem, recv_sem, device):
    return pltpu.make_async_remote_copy(
        src_ref=src,
        dst_ref=dst,
        send_sem=send_sem,
        recv_sem=recv_sem,
        device_id=device,
        device_id_type=MESH,
    )


def await_bytes(ref, sem):
    pltpu.make_async_copy(ref, ref, sem).wait()


class Gather:
    def __init__(self, buf, first, second, ring, number, src):
        a, b = first[0], second[0]
        column = [buf.at[:, (a + k) % SIDE] for k in (0, 3, 1, 2)]
        row = ring(number, buf.at[b], first, src, True)
        mine = ring(number + 1, column[0], second, src, False)
        before, after, far = [ring(number + 1 + k, column[k], second, None, False) for k in (1, 2, 3)]

        def come(way, onward):
            def step():
                row.forward_one(way)
                onward.start()

            return step

        def opposite():
            row.finish()
            far.start()

        self.steps = [
            [row.start, mine.start],
            [come(0, before), come(1, after), opposite, mine.forward],
            [before.forward, after.forward],
            [far.forward, mine.finish],
            [before.finish, after.finish, far.finish],
        ]
        self.rings = (row, mine, before, after, far)

    def drain(self):
        for r in self.rings:
            r.drain()


class Ring:
    def __init__(self, buf, here, right, left, far, sends, recvs, src=None, direct=False):
        self.buf, self.here, self.right, self.left = buf, here, right, left
        half = buf.shape[1] // 2
        before, after = (here + 3) % SIDE, (here + 1) % SIDE
        own = buf.at[here] if src is None else src
        mine = buf.at[here]
        self.sends, self.recvs = sends, recvs
        self.own = [
            remote(own, mine, sends, recvs.at[0], right),
            remote(own, mine, sends, recvs.at[1], left),
        ]
        low = buf.at[before, pl.ds(0, half)]
        high = buf.at[after, pl.ds(half, half)]
        self.pass_on = [
            remote(low, low, sends, recvs.at[2], right),
            remote(high, high, sends, recvs.at[2], left),
        ]
        self.direct = direct
        if direct:
            self.own.append(remote(own, mine, sends, recvs.at[2], far))

    def start(self):
        for copy in self.own:
            copy.start()

    def forward_one(self, way):
        self.own[way].wait_recv()
        if not self.direct:
            self.pass_on[way].start()

    def forward(self):
        self.forward_one(0)
        self.forward_one(1)

    def finish(self):
        await_bytes(self.buf.at[(self.here + 2) % SIDE], self.recvs.at[2])

    def drain(self):
        await_bytes(self.buf.at[pl.ds(0, SIDE - 1)], self.sends)


def kernel(
    n_tensor,
    tenant_hbm,
    dest_hbm,
    tokens_hbm,
    owner_hbm,
    x_hbm,
    g_hbm,
    ain_hbm,
    aout_hbm,
    dg_v,
    gin_v,
    gout_v,
    norm_ref,
    tenant_ref,
    dest_ref,
    tokens_ref,
    owner_ref,
    x_v,
    g_v,
    tab_in,
    tab_out,
    low_part,
    fac_part,
    low_got,
    fac_got,
    low_all,
    fac_all,
    term_in,
    term_out,
    pick,
    sum_in,
    sum_out,
    to_in,
    to_out,
    from_in,
    from_out,
    slot_send,
    slots,
    sq_own,
    sq_got,
    pos_own,
    pos_slot,
    ring_s,
    ring_r,
    z_s,
    z_r,
    slot_sem,
    own_s,
    own_r,
    sq_sem,
    loc,
):
    me = lax.axis_index("dp")
    t = lax.axis_index("tensor")
    y, x = me // SIDE, me % SIDE
    bt = BLK // n_tensor
    cd, cf = x_v.shape[1], g_v.shape[1]
    hd, hf = cd // 2, cf // 2

    ends = []

    def at_dp(yy, xx):
        return {"dp": yy * SIDE + xx}

    x_right, x_left = at_dp(y, (x + 1) % SIDE), at_dp(y, (x + 3) % SIDE)
    y_right, y_left = at_dp((y + 1) % SIDE, x), at_dp((y + 3) % SIDE, x)
    x_far, y_far = at_dp(y, (x + 2) % SIDE), at_dp((y + 2) % SIDE, x)
    along_x, along_y = (x, x_right, x_left, x_far), (y, y_right, y_left, y_far)

    load_x = pltpu.make_async_copy(x_hbm, x_v, loc.at[8])
    load_g = pltpu.make_async_copy(g_hbm, g_v, loc.at[9])
    in_cols = [ain_hbm.at[:, :, pl.ds(h * hd, hd)] for h in range(2)]
    out_cols = [aout_hbm.at[:, :, pl.ds(h * hf, hf)] for h in range(2)]
    places = [(y, x), (x, y)]
    own_tables = []
    for h in range(2):
        own_tables.append(
            pltpu.make_async_copy(in_cols[h], tab_in[h].at[places[h][0], places[h][1]], loc.at[2 + h])
        )
        own_tables.append(
            pltpu.make_async_copy(
                out_cols[h], tab_out[h].at[places[h][0], places[h][1]], loc.at[4 + h]
            )
        )
    plan = [
        pltpu.make_async_copy(tenant_hbm, tenant_ref, loc.at[0]),
        pltpu.make_async_copy(owner_hbm, owner_ref, loc.at[1]),
        pltpu.make_async_copy(dest_hbm, dest_ref, loc.at[6]),
        pltpu.make_async_copy(tokens_hbm, tokens_ref, loc.at[7]),
    ]
    for copy in plan + own_tables:
        copy.start()
    load_x.start()
    load_g.start()

    barrier = pltpu.get_barrier_semaphore()

    def greet_dp(k, _):
        pl.semaphore_signal(
            barrier, inc=1, device_id={"dp": (me + k) % GROUPS}, device_id_type=MESH
        )
        return 0

    def greet_tensor(k, _):
        pl.semaphore_signal(
            barrier, inc=1, device_id={"tensor": (t + k) % n_tensor}, device_id_type=MESH
        )
        return 0

    lax.fori_loop(1, GROUPS, greet_dp, 0)
    lax.fori_loop(1, n_tensor, greet_tensor, 0)

    def place_of(block):
        return owner_ref[tenant_ref[block]]

    def own_places(b, _):
        pos_own[b] = place_of(me * BLK + b)
        return 0

    for copy in plan:
        copy.wait()
    lax.fori_loop(0, BLK, own_places, 0)
    pl.semaphore_wait(barrier, GROUPS - 1 + n_tensor - 1)

    def slot_places(s, _):
        one, two = jnp.int32(-1), jnp.int32(-1)
        for i in range(BLK):
            b = s * BLK + i
            hit = dest_ref[b] == me
            p = place_of(b)
            two = jnp.where(hit & (one >= 0), p, two)
            one = jnp.where(hit & (one < 0), p, one)
        pos_slot[2 * s] = jnp.maximum(one, 0)
        pos_slot[2 * s + 1] = jnp.maximum(two, 0)
        return 0

    def slot_tables():
        lax.fori_loop(0, GROUPS, slot_places, 0)

    def choose(q, _):
        lane = lax.broadcasted_iota(jnp.int32, (8, 128), 1)
        wide = (SIDE * OWN * R, 128)
        row = lax.broadcasted_iota(jnp.int32, wide, 0)
        same = (row & (R - 1)) == (lax.broadcasted_iota(jnp.int32, wide, 1) & (R - 1))
        tall = row >> 4
        g, first_blk = q // 2, (q % 2) * 8
        for h in range(2):
            group = y * SIDE + g if h == 0 else g * SIDE + x
            want = jnp.full((8, 128), -1, jnp.int32)
            for i in range(8):
                p = place_of(group * BLK + first_blk + i)
                if h == 0:
                    local = jnp.where(((p >> 2) & 3) == x, ((p >> 4) << 2) | (p & 3), -1)
                else:
                    local = jnp.where((p >> 4) == y, p & 15, -1)
                want = jnp.where((lane >> 4) == i, local, want)
            hit = (tall == want[0:1]) & same
            pick[h][:, pl.ds(pl.multiple_of(q * 128, 128), 128)] = jnp.where(hit, 1.0, 0.0).astype(BF16)
        return 0

    def choose_all():
        lax.fori_loop(0, 2 * SIDE, choose, 0)

    def find(k, found):
        at = owner_ref[k] - me * OWN
        return tuple(jnp.where(at == j, tokens_ref[k], found[j]) for j in range(OWN))

    def owned_weights():
        found = lax.fori_loop(0, owner_ref.shape[0], find, (jnp.int32(1),) * OWN)
        return [1.0 / jnp.full((1, 128), f, jnp.int32).astype(F32) for f in found]

    def ring(number, buf, along, src=None, direct=False):
        return Ring(buf, *along, ring_s.at[number], ring_r.at[number], src, direct)

    first, second = [along_x, along_y], [along_y, along_x]
    tab_in_ag = [Gather(tab_in[h], first[h], second[h], ring, 5 * h, in_cols[h]) for h in range(2)]
    tab_out_ag = [
        Gather(tab_out[h], first[h], second[h], ring, 10 + 5 * h, out_cols[h]) for h in range(2)
    ]

    def deep(gathers, depth):
        for part in range(len(gathers[0].steps[depth])):
            for gather in gathers:
                gather.steps[depth][part]()

    def partial_products(table, rows_v, half, part):
        def one(b, _):
            p = pos_own[b]
            rows = rows_v[pl.ds(pl.multiple_of(b * ROWS, ROWS), ROWS), :]
            tab_a = table[0][p >> 4, (p >> 2) & 3, p & 3]
            tab_b = table[1][(p >> 2) & 3, p >> 4, p & 3]
            nt = (((1,), (1,)), ((), ()))
            part[b] = lax.dot_general(
                tab_a, rows[:, :half], nt, preferred_element_type=F32
            ) + lax.dot_general(tab_b, rows[:, half:], nt, preferred_element_type=F32)
            return 0

        lax.fori_loop(0, BLK, one, 0, unroll=2)

    def reduce_copy(part, got, number, k):
        to = (t + k) % n_tensor
        return remote(
            part.at[pl.ds(to * bt, bt)],
            got.at[k],
            z_s.at[number],
            z_r.at[number],
            {"tensor": to},
        )

    def spread_copy(full, number, k):
        mine = full.at[pl.ds(t * bt, bt)]
        return remote(
            mine, mine, z_s.at[number], z_r.at[number], {"tensor": (t + k) % n_tensor}
        )

    def over_tensor(do):
        lax.fori_loop(1, n_tensor, lambda k, _: (do(k), 0)[1], 0)

    def send_parts(part, got, number):
        over_tensor(lambda k: reduce_copy(part, got, number, k).start())
        ends.append(lambda: await_bytes(got.at[pl.ds(1, n_tensor - 1)], z_s.at[number]))

    def add_parts(part, got, full, number, scale):
        await_bytes(got.at[pl.ds(1, n_tensor - 1)], z_r.at[number])
        total = lax.fori_loop(1, n_tensor, lambda k, acc: acc + got[k], part[pl.ds(t * bt, bt)])
        full[pl.ds(t * bt, bt)] = (scale * total).astype(BF16)
        over_tensor(lambda k: spread_copy(full, number + 1, k).start())
        ends.append(lambda: await_bytes(full.at[pl.ds(0, BLK - bt)], z_s.at[number + 1]))

    def take_spread(full, number):
        await_bytes(full.at[pl.ds(0, BLK - bt)], z_r.at[number])

    def terms(h, factor, rows_v, half, out):
        def one(b, _):
            rows = rows_v[pl.ds(pl.multiple_of(b * ROWS, ROWS), ROWS), pl.ds(h * half, half)]
            out[h][first[h][0], b] = jnp.dot(
                factor[b], rows, preferred_element_type=F32
            ).astype(BF16)
            return 0

        lax.fori_loop(0, BLK, one, 0, unroll=2)

    for gathers in (tab_in_ag, tab_out_ag):
        ends.extend(g.drain for g in gathers)
    deep(tab_in_ag, 0)
    deep(tab_out_ag, 0)
    slot_tables()
    deep(tab_in_ag, 1)
    deep(tab_in_ag, 2)
    deep(tab_in_ag, 3)
    deep(tab_in_ag, 4)
    for copy in own_tables:
        copy.wait()
    load_x.wait()
    partial_products(tab_in, x_v, hd, low_part)
    send_parts(low_part, low_got, 0)
    deep(tab_out_ag, 1)
    deep(tab_out_ag, 2)
    choose_all()
    add_parts(low_part, low_got, low_all, 0, 1.0)
    deep(tab_out_ag, 3)
    deep(tab_out_ag, 4)
    load_g.wait()
    partial_products(tab_out, g_v, hf, fac_part)
    send_parts(fac_part, fac_got, 2)
    take_spread(low_all, 1)
    term_out_1 = [ring(20 + h, term_out[h], first[h], None, False) for h in range(2)]
    for h in range(2):
        terms(h, low_all, g_v, hf, term_out)
        term_out_1[h].start()
        ends.append(term_out_1[h].drain)
    add_parts(fac_part, fac_got, fac_all, 2, 2.0)
    for r in term_out_1:
        r.forward()
    weight = owned_weights()
    take_spread(fac_all, 3)
    term_in_1 = [ring(22 + h, term_in[h], first[h], None, False) for h in range(2)]
    for h in range(2):
        terms(h, fac_all, x_v, hd, term_in)
        term_in_1[h].start()
        ends.append(term_in_1[h].drain)

    def slot_copy(k):
        to = (me + k) % GROUPS
        return remote(slot_send.at[k], slots.at[me], slot_sem.at[0], slot_sem.at[1], {"dp": to})

    def blocks_for(group):
        one, two = jnp.int32(-1), jnp.int32(-1)
        for i in range(BLK):
            hit = dest_ref[me * BLK + i] == group
            two = jnp.where(hit & (one >= 0), i, two)
            one = jnp.where(hit & (one < 0), i, one)
        return one, two

    def masked(i):
        live = jnp.where(i >= 0, 1.0, 0.0).astype(F32)
        return (fac_all[jnp.maximum(i, 0)].astype(F32) * live).astype(BF16)

    def pack(k, _):
        one, two = blocks_for((me + k) % GROUPS)
        slot_send[k, 0] = masked(one)
        slot_send[k, 1] = masked(two)
        slot_copy(k).start()
        return 0

    lax.fori_loop(1, GROUPS, pack, 0)

    ends.append(lambda: await_bytes(slots.at[pl.ds(0, GROUPS - 1)], slot_sem.at[0]))
    one, two = blocks_for(me)
    slots[me, 0] = masked(one)
    slots[me, 1] = masked(two)

    def owner_copies(number, h, sends, lands):
        here = second[h][0]
        copies = []
        for k in range(1, SIDE):
            to = (here + k) % SIDE
            device = at_dp(to, x) if h == 0 else at_dp(y, to)
            copies.append(
                remote(
                    sends.at[to],
                    lands.at[k - 1],
                    own_s.at[number],
                    own_r.at[number],
                    device,
                )
            )
        return copies

    def add_terms(h, term, total, sends):
        cols = total.shape[1]
        step = min(cols, 256)
        rows = SIDE * OWN * R

        def one(c, _):
            where = pl.ds(pl.multiple_of(c * step, step), step)
            block = term[:, :, :, where].reshape(SIDE * BLK * R, step)
            out = jnp.dot(pick[h][...], block, preferred_element_type=F32)
            total[:, where] = out
            sends[:, :, where] = out.reshape(SIDE, OWN * R, step).astype(BF16)
            return 0

        lax.fori_loop(0, cols // step, one, 0)

    def own_sum(h, total, lands, result, scale, half):
        here = second[h][0]
        kept = total[pl.ds(pl.multiple_of(here * OWN * R, OWN * R), OWN * R), :]
        for k in range(SIDE - 1):
            kept = kept + lands[k].astype(F32)
        squares = []
        for j in range(OWN):
            piece = kept[j * R : (j + 1) * R] * scale[j]
            result[j, :, pl.ds(h * half, half)] = piece
            squares.append(jnp.sum(piece * piece, axis=0, keepdims=True))
        return squares

    out_own = [owner_copies(h, h, to_out[h], from_out[h]) for h in range(2)]
    in_own = [owner_copies(2 + h, h, to_in[h], from_in[h]) for h in range(2)]
    for h in range(2):
        term_out_1[h].finish()
        add_terms(h, term_out[h], sum_out[h], to_out[h])
        for copy in out_own[h]:
            copy.start()
    for r in term_in_1:
        r.forward()

    await_bytes(slots.at[pl.ds(0, GROUPS - 1)], slot_sem.at[1])

    def apply_factor(i, _):
        p = pos_slot[i]
        factor = slots[i // 2, i % 2]
        rows = pl.ds(pl.multiple_of(i * ROWS, ROWS), ROWS)
        tn = (((0,), (0,)), ((), ()))
        dg_v[rows, :hd] = lax.dot_general(
            factor, tab_in[0][p >> 4, (p >> 2) & 3, p & 3], tn, preferred_element_type=F32
        ).astype(BF16)
        dg_v[rows, hd:] = lax.dot_general(
            factor, tab_in[1][(p >> 2) & 3, p >> 4, p & 3], tn, preferred_element_type=F32
        ).astype(BF16)
        return 0

    lax.fori_loop(0, 2 * GROUPS, apply_factor, 0, unroll=4)

    for h in range(2):
        term_in_1[h].finish()
        add_terms(h, term_in[h], sum_in[h], to_in[h])
        for copy in in_own[h]:
            copy.start()

    def weigh(half, by):
        return [jnp.tile(by * w, (1, half // 128)) for w in weight]

    for h in range(2):
        await_bytes(from_out[h], own_r.at[h])
    parts = [own_sum(h, sum_out[h], from_out[h], gout_v, weigh(hf, 2.0), hf) for h in range(2)]
    for h in range(2):
        await_bytes(from_in[h], own_r.at[2 + h])
    parts += [own_sum(h, sum_in[h], from_in[h], gin_v, weigh(hd, 1.0), hd) for h in range(2)]

    for h in range(2):
        ends.append(functools.partial(await_bytes, from_out[h], own_s.at[h]))
        ends.append(functools.partial(await_bytes, from_in[h], own_s.at[2 + h]))

    row8 = lax.broadcasted_iota(jnp.int32, (8, 128), 0)
    square = jnp.zeros((8, 128), F32)
    for j in range(OWN):
        one_sum = jnp.zeros((1, 128), F32)
        for part in parts:
            for c in range(part[j].shape[1] // 128):
                one_sum = one_sum + part[j][:, c * 128 : (c + 1) * 128]
        square = jnp.where(row8 == j, one_sum, square)
    sq_own[...] = square

    def square_copy(k):
        return remote(
            sq_own, sq_got.at[k], sq_sem.at[0], sq_sem.at[1], {"tensor": (t + k) % n_tensor}
        )

    over_tensor(lambda k: square_copy(k).start())
    ends.append(lambda: await_bytes(sq_got.at[pl.ds(1, n_tensor - 1)], sq_sem.at[0]))
    await_bytes(sq_got.at[pl.ds(1, n_tensor - 1)], sq_sem.at[1])
    total = lax.fori_loop(1, n_tensor, lambda k, acc: acc + sq_got[k], sq_own[...])
    norm_ref[...] = jnp.sqrt(jnp.broadcast_to(jnp.sum(total, axis=1, keepdims=True), (8, 128)))

    for end in ends:
        end()


def place(dg, gin, gout, norms, dg_to, gin_to, gout_to, norms_to, sems):
    quarter = dg.shape[0] // 4
    moves = [(gin, gin_to), (gout, gout_to)]
    for i in range(4):
        rows = pl.ds(i * quarter, quarter)
        moves.append((dg.at[rows], dg_to.at[rows]))
    copies = [pltpu.make_async_copy(a, b, sems.at[i]) for i, (a, b) in enumerate(moves)]
    for copy in copies:
        copy.start()
    for j in range(OWN):
        norms_to[j] = norms[j, 0]
    for copy in copies:
        copy.wait()


def per_device(
    hidden_in, grad_gate, adapter_in, adapter_out, block_tenant, block_dest, tenant_tokens, tenant_owner
):
    n_tensor = lax.axis_size("tensor")
    bt = BLK // n_tensor
    cd, cf = hidden_in.shape[1], grad_gate.shape[1]
    hd, hf = cd // 2, cf // 2
    wide = SIDE * OWN * R

    def pair(shape, dtype):
        return [pltpu.VMEM(shape, dtype), pltpu.VMEM(shape, dtype)]

    dma = pltpu.SemaphoreType.DMA
    smem = pl.BlockSpec(memory_space=pltpu.SMEM)
    hbm = pl.BlockSpec(memory_space=pltpu.HBM)
    vmem = pl.BlockSpec(memory_space=pltpu.VMEM)
    scratch = [
        pltpu.SMEM(block_tenant.shape, jnp.int32),
        pltpu.SMEM(block_tenant.shape, jnp.int32),
        pltpu.SMEM(tenant_tokens.shape, jnp.int32),
        pltpu.SMEM(tenant_owner.shape, jnp.int32),
        pltpu.VMEM(hidden_in.shape, BF16),
        pltpu.VMEM(grad_gate.shape, BF16),
        pair((SIDE, SIDE, OWN, R, hd), BF16),
        pair((SIDE, SIDE, OWN, R, hf), BF16),
        pltpu.VMEM((BLK, R, ROWS), F32),
        pltpu.VMEM((BLK, R, ROWS), F32),
        pltpu.VMEM((n_tensor, bt, R, ROWS), F32),
        pltpu.VMEM((n_tensor, bt, R, ROWS), F32),
        pltpu.VMEM((BLK, R, ROWS), BF16),
        pltpu.VMEM((BLK, R, ROWS), BF16),
        pair((SIDE, BLK, R, hd), BF16),
        pair((SIDE, BLK, R, hf), BF16),
        pair((wide, SIDE * BLK * R), BF16),
        pair((wide, hd), F32),
        pair((wide, hf), F32),
        pair((SIDE, OWN * R, hd), BF16),
        pair((SIDE, OWN * R, hf), BF16),
        pair((SIDE - 1, OWN * R, hd), BF16),
        pair((SIDE - 1, OWN * R, hf), BF16),
        pltpu.VMEM((GROUPS, 2, R, ROWS), BF16),
        pltpu.VMEM((GROUPS, 2, R, ROWS), BF16),
        pltpu.VMEM((8, 128), F32),
        pltpu.VMEM((n_tensor, 8, 128), F32),
        pltpu.SMEM((BLK,), jnp.int32),
        pltpu.SMEM((2 * GROUPS,), jnp.int32),
        dma((24,)),
        dma((24, 3)),
        dma((4,)),
        dma((4,)),
        dma((2,)),
        dma((4,)),
        dma((4,)),
        dma((2,)),
        dma((10,)),
    ]
    results = pl.pallas_call(
        functools.partial(kernel, n_tensor),
        out_shape=(
            jax.ShapeDtypeStruct((GROUPS * 2 * ROWS, cd), BF16),
            jax.ShapeDtypeStruct((OWN, R, cd), F32),
            jax.ShapeDtypeStruct((OWN, R, cf), F32),
            jax.ShapeDtypeStruct((8, 128), F32),
        ),
        in_specs=[hbm] * 8,
        out_specs=(vmem,) * 4,
        scratch_shapes=scratch,
        compiler_params=pltpu.CompilerParams(
            collective_id=0, has_side_effects=True, vmem_limit_bytes=40 * 1024 * 1024
        ),
    )(
        *(
            pltpu.with_memory_space_constraint(a, pltpu.HBM)
            for a in (
                block_tenant,
                block_dest.reshape(-1),
                tenant_tokens,
                tenant_owner,
                hidden_in,
                grad_gate,
                adapter_in,
                adapter_out,
            )
        )
    )
    return pl.pallas_call(
        place,
        out_shape=(
            jax.ShapeDtypeStruct((GROUPS * 2 * ROWS, cd), BF16),
            jax.ShapeDtypeStruct((OWN, R, cd), F32),
            jax.ShapeDtypeStruct((OWN, R, cf), F32),
            jax.ShapeDtypeStruct((OWN,), F32),
        ),
        in_specs=[vmem, vmem, vmem, smem],
        out_specs=(hbm, hbm, hbm, smem),
        scratch_shapes=[dma((6,))],
        compiler_params=pltpu.CompilerParams(vmem_limit_bytes=16 * 1024 * 1024),
    )(*results)


def solution(mesh):
    return jax.shard_map(
        per_device,
        mesh=mesh,
        in_specs=(
            P("dp", "tensor"),
            P("dp", "tensor"),
            P("dp", None, "tensor"),
            P("dp", None, "tensor"),
            P(),
            P(),
            P(),
            P(),
        ),
        out_specs=(P("dp", "tensor"), P("dp", None, "tensor"), P("dp", None, "tensor"), P("dp")),
        check_vma=False,
    )
```

```python
import functools

import jax
import jax.numpy as jnp
from jax import lax
from jax.experimental import pallas as pl
from jax.experimental.pallas import tpu as pltpu
from jax.sharding import PartitionSpec as P

SIDE = 4
R = 16
ROWS = 128
BLK = 16
OWN = 4
GROUPS = SIDE * SIDE
MESH = pl.DeviceIdType.MESH
BF16 = jnp.bfloat16
F32 = jnp.float32


def remote(src, dst, send_sem, recv_sem, device):
    return pltpu.make_async_remote_copy(
        src_ref=src,
        dst_ref=dst,
        send_sem=send_sem,
        recv_sem=recv_sem,
        device_id=device,
        device_id_type=MESH,
    )


def await_bytes(ref, sem):
    pltpu.make_async_copy(ref, ref, sem).wait()


class Gather:
    def __init__(self, buf, first, second, ring, number, src):
        a, b = first[0], second[0]
        column = [buf.at[:, (a + k) % SIDE] for k in (0, 3, 1, 2)]
        row = ring(number, buf.at[b], first, src, True)
        mine = ring(number + 1, column[0], second, src, False)
        before, after, far = [ring(number + 1 + k, column[k], second, None, False) for k in (1, 2, 3)]

        def come(way, onward):
            def step():
                row.forward_one(way)
                onward.start()

            return step

        def opposite():
            row.finish()
            far.start()

        self.steps = [
            [row.start, mine.start],
            [come(0, before), come(1, after), opposite, mine.forward],
            [before.forward, after.forward],
            [far.forward, mine.finish],
            [before.finish, after.finish, far.finish],
        ]
        self.rings = (row, mine, before, after, far)

    def drain(self):
        for r in self.rings:
            r.drain()


class Ring:
    def __init__(self, buf, here, right, left, far, sends, recvs, src=None, direct=False):
        self.buf, self.here, self.right, self.left = buf, here, right, left
        half = buf.shape[1] // 2
        before, after = (here + 3) % SIDE, (here + 1) % SIDE
        own = buf.at[here] if src is None else src
        mine = buf.at[here]
        self.sends, self.recvs = sends, recvs
        self.own = [
            remote(own, mine, sends, recvs.at[0], right),
            remote(own, mine, sends, recvs.at[1], left),
        ]
        low = buf.at[before, pl.ds(0, half)]
        high = buf.at[after, pl.ds(half, half)]
        self.pass_on = [
            remote(low, low, sends, recvs.at[2], right),
            remote(high, high, sends, recvs.at[2], left),
        ]
        self.direct = direct
        if direct:
            self.own.append(remote(own, mine, sends, recvs.at[2], far))

    def start(self):
        for copy in self.own:
            copy.start()

    def forward_one(self, way):
        self.own[way].wait_recv()
        if not self.direct:
            self.pass_on[way].start()

    def forward(self):
        self.forward_one(0)
        self.forward_one(1)

    def finish(self):
        await_bytes(self.buf.at[(self.here + 2) % SIDE], self.recvs.at[2])

    def drain(self):
        await_bytes(self.buf.at[pl.ds(0, SIDE - 1)], self.sends)


def kernel(
    n_tensor,
    tenant_hbm,
    dest_hbm,
    tokens_hbm,
    owner_hbm,
    x_hbm,
    g_hbm,
    ain_hbm,
    aout_hbm,
    dg_v,
    gin_v,
    gout_v,
    norm_ref,
    tenant_ref,
    dest_ref,
    tokens_ref,
    owner_ref,
    x_v,
    g_v,
    tab_in,
    tab_out,
    low_part,
    fac_part,
    low_got,
    fac_got,
    low_all,
    fac_all,
    term_in,
    term_out,
    pick,
    sum_in,
    sum_out,
    to_in,
    to_out,
    from_in,
    from_out,
    slot_send,
    slots,
    sq_own,
    sq_got,
    pos_own,
    pos_slot,
    ring_s,
    ring_r,
    z_s,
    z_r,
    slot_sem,
    own_s,
    own_r,
    sq_sem,
    loc,
):
    me = lax.axis_index("dp")
    t = lax.axis_index("tensor")
    y, x = me // SIDE, me % SIDE
    bt = BLK // n_tensor
    cd, cf = x_v.shape[1], g_v.shape[1]
    hd, hf = cd // 2, cf // 2

    ends = []

    def at_dp(yy, xx):
        return {"dp": yy * SIDE + xx}

    x_right, x_left = at_dp(y, (x + 1) % SIDE), at_dp(y, (x + 3) % SIDE)
    y_right, y_left = at_dp((y + 1) % SIDE, x), at_dp((y + 3) % SIDE, x)
    x_far, y_far = at_dp(y, (x + 2) % SIDE), at_dp((y + 2) % SIDE, x)
    along_x, along_y = (x, x_right, x_left, x_far), (y, y_right, y_left, y_far)

    load_x = pltpu.make_async_copy(x_hbm, x_v, loc.at[8])
    load_g = pltpu.make_async_copy(g_hbm, g_v, loc.at[9])
    in_cols = [ain_hbm.at[:, :, pl.ds(h * hd, hd)] for h in range(2)]
    out_cols = [aout_hbm.at[:, :, pl.ds(h * hf, hf)] for h in range(2)]
    places = [(y, x), (x, y)]
    own_tables = []
    for h in range(2):
        own_tables.append(
            pltpu.make_async_copy(in_cols[h], tab_in[h].at[places[h][0], places[h][1]], loc.at[2 + h])
        )
        own_tables.append(
            pltpu.make_async_copy(
                out_cols[h], tab_out[h].at[places[h][0], places[h][1]], loc.at[4 + h]
            )
        )
    plan = [
        pltpu.make_async_copy(tenant_hbm, tenant_ref, loc.at[0]),
        pltpu.make_async_copy(owner_hbm, owner_ref, loc.at[1]),
        pltpu.make_async_copy(dest_hbm, dest_ref, loc.at[6]),
        pltpu.make_async_copy(tokens_hbm, tokens_ref, loc.at[7]),
    ]
    for copy in plan + own_tables:
        copy.start()
    load_x.start()
    load_g.start()

    barrier = pltpu.get_barrier_semaphore()

    def greet_dp(k, _):
        pl.semaphore_signal(
            barrier, inc=1, device_id={"dp": (me + k) % GROUPS}, device_id_type=MESH
        )
        return 0

    def greet_tensor(k, _):
        pl.semaphore_signal(
            barrier, inc=1, device_id={"tensor": (t + k) % n_tensor}, device_id_type=MESH
        )
        return 0

    lax.fori_loop(1, GROUPS, greet_dp, 0)
    lax.fori_loop(1, n_tensor, greet_tensor, 0)

    def place_of(block):
        return owner_ref[tenant_ref[block]]

    def own_places(b, _):
        pos_own[b] = place_of(me * BLK + b)
        return 0

    for copy in plan:
        copy.wait()
    lax.fori_loop(0, BLK, own_places, 0)
    pl.semaphore_wait(barrier, GROUPS - 1 + n_tensor - 1)

    def slot_places(s, _):
        one, two = jnp.int32(-1), jnp.int32(-1)
        for i in range(BLK):
            b = s * BLK + i
            hit = dest_ref[b] == me
            p = place_of(b)
            two = jnp.where(hit & (one >= 0), p, two)
            one = jnp.where(hit & (one < 0), p, one)
        pos_slot[2 * s] = jnp.maximum(one, 0)
        pos_slot[2 * s + 1] = jnp.maximum(two, 0)
        return 0

    def slot_tables():
        lax.fori_loop(0, GROUPS, slot_places, 0)

    def choose(q, _):
        lane = lax.broadcasted_iota(jnp.int32, (8, 128), 1)
        wide = (SIDE * OWN * R, 128)
        row = lax.broadcasted_iota(jnp.int32, wide, 0)
        same = (row & (R - 1)) == (lax.broadcasted_iota(jnp.int32, wide, 1) & (R - 1))
        tall = row >> 4
        g, first_blk = q // 2, (q % 2) * 8
        for h in range(2):
            group = y * SIDE + g if h == 0 else g * SIDE + x
            want = jnp.full((8, 128), -1, jnp.int32)
            for i in range(8):
                p = place_of(group * BLK + first_blk + i)
                if h == 0:
                    local = jnp.where(((p >> 2) & 3) == x, ((p >> 4) << 2) | (p & 3), -1)
                else:
                    local = jnp.where((p >> 4) == y, p & 15, -1)
                want = jnp.where((lane >> 4) == i, local, want)
            hit = (tall == want[0:1]) & same
            pick[h][:, pl.ds(pl.multiple_of(q * 128, 128), 128)] = jnp.where(hit, 1.0, 0.0).astype(BF16)
        return 0

    def choose_all():
        lax.fori_loop(0, 2 * SIDE, choose, 0)

    def find(k, found):
        at = owner_ref[k] - me * OWN
        return tuple(jnp.where(at == j, tokens_ref[k], found[j]) for j in range(OWN))

    def owned_weights():
        found = lax.fori_loop(0, owner_ref.shape[0], find, (jnp.int32(1),) * OWN)
        return [1.0 / jnp.full((1, 128), f, jnp.int32).astype(F32) for f in found]

    def ring(number, buf, along, src=None, direct=False):
        return Ring(buf, *along, ring_s.at[number], ring_r.at[number], src, direct)

    first, second = [along_x, along_y], [along_y, along_x]
    tab_in_ag = [Gather(tab_in[h], first[h], second[h], ring, 5 * h, in_cols[h]) for h in range(2)]
    tab_out_ag = [
        Gather(tab_out[h], first[h], second[h], ring, 10 + 5 * h, out_cols[h]) for h in range(2)
    ]

    def deep(gathers, depth):
        for part in range(len(gathers[0].steps[depth])):
            for gather in gathers:
                gather.steps[depth][part]()

    def partial_products(table, rows_v, half, part):
        def one(b, _):
            p = pos_own[b]
            rows = rows_v[pl.ds(pl.multiple_of(b * ROWS, ROWS), ROWS), :]
            tab_a = table[0][p >> 4, (p >> 2) & 3, p & 3]
            tab_b = table[1][(p >> 2) & 3, p >> 4, p & 3]
            nt = (((1,), (1,)), ((), ()))
            part[b] = lax.dot_general(
                tab_a, rows[:, :half], nt, preferred_element_type=F32
            ) + lax.dot_general(tab_b, rows[:, half:], nt, preferred_element_type=F32)
            return 0

        lax.fori_loop(0, BLK, one, 0, unroll=2)

    def reduce_copy(part, got, number, k):
        to = (t + k) % n_tensor
        return remote(
            part.at[pl.ds(to * bt, bt)],
            got.at[k],
            z_s.at[number],
            z_r.at[number],
            {"tensor": to},
        )

    def spread_copy(full, number, k):
        mine = full.at[pl.ds(t * bt, bt)]
        return remote(
            mine, mine, z_s.at[number], z_r.at[number], {"tensor": (t + k) % n_tensor}
        )

    def over_tensor(do):
        lax.fori_loop(1, n_tensor, lambda k, _: (do(k), 0)[1], 0)

    def send_parts(part, got, number):
        over_tensor(lambda k: reduce_copy(part, got, number, k).start())
        ends.append(lambda: await_bytes(got.at[pl.ds(1, n_tensor - 1)], z_s.at[number]))

    def add_parts(part, got, full, number, scale):
        await_bytes(got.at[pl.ds(1, n_tensor - 1)], z_r.at[number])
        total = lax.fori_loop(1, n_tensor, lambda k, acc: acc + got[k], part[pl.ds(t * bt, bt)])
        full[pl.ds(t * bt, bt)] = (scale * total).astype(BF16)
        over_tensor(lambda k: spread_copy(full, number + 1, k).start())
        ends.append(lambda: await_bytes(full.at[pl.ds(0, BLK - bt)], z_s.at[number + 1]))

    def take_spread(full, number):
        await_bytes(full.at[pl.ds(0, BLK - bt)], z_r.at[number])

    def terms(h, factor, rows_v, half, out):
        def one(b, _):
            rows = rows_v[pl.ds(pl.multiple_of(b * ROWS, ROWS), ROWS), pl.ds(h * half, half)]
            out[h][first[h][0], b] = jnp.dot(
                factor[b], rows, preferred_element_type=F32
            ).astype(BF16)
            return 0

        lax.fori_loop(0, BLK, one, 0, unroll=2)

    for gathers in (tab_in_ag, tab_out_ag):
        ends.extend(g.drain for g in gathers)
    deep(tab_in_ag, 0)
    deep(tab_out_ag, 0)
    slot_tables()
    deep(tab_in_ag, 1)
    deep(tab_in_ag, 2)
    deep(tab_in_ag, 3)
    deep(tab_in_ag, 4)
    for copy in own_tables:
        copy.wait()
    load_x.wait()
    partial_products(tab_in, x_v, hd, low_part)
    send_parts(low_part, low_got, 0)
    deep(tab_out_ag, 1)
    deep(tab_out_ag, 2)
    choose_all()
    add_parts(low_part, low_got, low_all, 0, 1.0)
    deep(tab_out_ag, 3)
    deep(tab_out_ag, 4)
    load_g.wait()
    partial_products(tab_out, g_v, hf, fac_part)
    send_parts(fac_part, fac_got, 2)
    take_spread(low_all, 1)
    term_out_1 = [ring(20 + h, term_out[h], first[h], None, False) for h in range(2)]
    for h in range(2):
        terms(h, low_all, g_v, hf, term_out)
        term_out_1[h].start()
        ends.append(term_out_1[h].drain)
    add_parts(fac_part, fac_got, fac_all, 2, 2.0)
    for r in term_out_1:
        r.forward()
    weight = owned_weights()
    take_spread(fac_all, 3)
    term_in_1 = [ring(22 + h, term_in[h], first[h], None, False) for h in range(2)]
    for h in range(2):
        terms(h, fac_all, x_v, hd, term_in)
        term_in_1[h].start()
        ends.append(term_in_1[h].drain)

    def slot_copy(k):
        to = (me + k) % GROUPS
        return remote(slot_send.at[k], slots.at[me], slot_sem.at[0], slot_sem.at[1], {"dp": to})

    def blocks_for(group):
        one, two = jnp.int32(-1), jnp.int32(-1)
        for i in range(BLK):
            hit = dest_ref[me * BLK + i] == group
            two = jnp.where(hit & (one >= 0), i, two)
            one = jnp.where(hit & (one < 0), i, one)
        return one, two

    def masked(i):
        live = jnp.where(i >= 0, 1.0, 0.0).astype(F32)
        return (fac_all[jnp.maximum(i, 0)].astype(F32) * live).astype(BF16)

    def pack(k, _):
        one, two = blocks_for((me + k) % GROUPS)
        slot_send[k, 0] = masked(one)
        slot_send[k, 1] = masked(two)
        slot_copy(k).start()
        return 0

    def owner_copies(number, h, sends, lands):
        here = second[h][0]
        copies = []
        for k in range(1, SIDE):
            to = (here + k) % SIDE
            device = at_dp(to, x) if h == 0 else at_dp(y, to)
            copies.append(
                remote(
                    sends.at[to],
                    lands.at[k - 1],
                    own_s.at[number],
                    own_r.at[number],
                    device,
                )
            )
        return copies

    def add_terms(h, term, total, sends):
        cols = total.shape[1]
        step = min(cols, 256)
        rows = SIDE * OWN * R

        def one(c, _):
            where = pl.ds(pl.multiple_of(c * step, step), step)
            block = term[:, :, :, where].reshape(SIDE * BLK * R, step)
            out = jnp.dot(pick[h][...], block, preferred_element_type=F32)
            total[:, where] = out
            sends[:, :, where] = out.reshape(SIDE, OWN * R, step).astype(BF16)
            return 0

        lax.fori_loop(0, cols // step, one, 0)

    def own_sum(h, total, lands, result, scale, half):
        here = second[h][0]
        kept = total[pl.ds(pl.multiple_of(here * OWN * R, OWN * R), OWN * R), :]
        for k in range(SIDE - 1):
            kept = kept + lands[k].astype(F32)
        squares = []
        for j in range(OWN):
            piece = kept[j * R : (j + 1) * R] * scale[j]
            result[j, :, pl.ds(h * half, half)] = piece
            squares.append(jnp.sum(piece * piece, axis=0, keepdims=True))
        return squares

    out_own = [owner_copies(h, h, to_out[h], from_out[h]) for h in range(2)]
    in_own = [owner_copies(2 + h, h, to_in[h], from_in[h]) for h in range(2)]
    for h in range(2):
        term_out_1[h].finish()
        add_terms(h, term_out[h], sum_out[h], to_out[h])
    for r in term_in_1:
        r.forward()
    lax.fori_loop(1, GROUPS, pack, 0)

    ends.append(lambda: await_bytes(slots.at[pl.ds(0, GROUPS - 1)], slot_sem.at[0]))
    one, two = blocks_for(me)
    slots[me, 0] = masked(one)
    slots[me, 1] = masked(two)

    for h in range(2):
        for copy in out_own[h]:
            copy.start()

    for h in range(2):
        term_in_1[h].finish()
        add_terms(h, term_in[h], sum_in[h], to_in[h])
        for copy in in_own[h]:
            copy.start()

    await_bytes(slots.at[pl.ds(0, GROUPS - 1)], slot_sem.at[1])

    def apply_factor(i, _):
        p = pos_slot[i]
        factor = slots[i // 2, i % 2]
        rows = pl.ds(pl.multiple_of(i * ROWS, ROWS), ROWS)
        tn = (((0,), (0,)), ((), ()))
        dg_v[rows, :hd] = lax.dot_general(
            factor, tab_in[0][p >> 4, (p >> 2) & 3, p & 3], tn, preferred_element_type=F32
        ).astype(BF16)
        dg_v[rows, hd:] = lax.dot_general(
            factor, tab_in[1][(p >> 2) & 3, p >> 4, p & 3], tn, preferred_element_type=F32
        ).astype(BF16)
        return 0

    lax.fori_loop(0, 2 * GROUPS, apply_factor, 0, unroll=4)

    def weigh(half, by):
        return [jnp.tile(by * w, (1, half // 128)) for w in weight]

    for h in range(2):
        await_bytes(from_out[h], own_r.at[h])
    parts = [own_sum(h, sum_out[h], from_out[h], gout_v, weigh(hf, 2.0), hf) for h in range(2)]
    for h in range(2):
        await_bytes(from_in[h], own_r.at[2 + h])
    parts += [own_sum(h, sum_in[h], from_in[h], gin_v, weigh(hd, 1.0), hd) for h in range(2)]

    for h in range(2):
        ends.append(functools.partial(await_bytes, from_out[h], own_s.at[h]))
        ends.append(functools.partial(await_bytes, from_in[h], own_s.at[2 + h]))

    row8 = lax.broadcasted_iota(jnp.int32, (8, 128), 0)
    square = jnp.zeros((8, 128), F32)
    for j in range(OWN):
        one_sum = jnp.zeros((1, 128), F32)
        for part in parts:
            for c in range(part[j].shape[1] // 128):
                one_sum = one_sum + part[j][:, c * 128 : (c + 1) * 128]
        square = jnp.where(row8 == j, one_sum, square)
    sq_own[...] = square

    def square_copy(k):
        return remote(
            sq_own, sq_got.at[k], sq_sem.at[0], sq_sem.at[1], {"tensor": (t + k) % n_tensor}
        )

    over_tensor(lambda k: square_copy(k).start())
    ends.append(lambda: await_bytes(sq_got.at[pl.ds(1, n_tensor - 1)], sq_sem.at[0]))
    await_bytes(sq_got.at[pl.ds(1, n_tensor - 1)], sq_sem.at[1])
    total = lax.fori_loop(1, n_tensor, lambda k, acc: acc + sq_got[k], sq_own[...])
    norm_ref[...] = jnp.sqrt(jnp.broadcast_to(jnp.sum(total, axis=1, keepdims=True), (8, 128)))

    for end in ends:
        end()


def place(dg, gin, gout, norms, dg_to, gin_to, gout_to, norms_to, sems):
    quarter = dg.shape[0] // 4
    moves = [(gin, gin_to), (gout, gout_to)]
    for i in range(4):
        rows = pl.ds(i * quarter, quarter)
        moves.append((dg.at[rows], dg_to.at[rows]))
    copies = [pltpu.make_async_copy(a, b, sems.at[i]) for i, (a, b) in enumerate(moves)]
    for copy in copies:
        copy.start()
    for j in range(OWN):
        norms_to[j] = norms[j, 0]
    for copy in copies:
        copy.wait()


def per_device(
    hidden_in, grad_gate, adapter_in, adapter_out, block_tenant, block_dest, tenant_tokens, tenant_owner
):
    n_tensor = lax.axis_size("tensor")
    bt = BLK // n_tensor
    cd, cf = hidden_in.shape[1], grad_gate.shape[1]
    hd, hf = cd // 2, cf // 2
    wide = SIDE * OWN * R

    def pair(shape, dtype):
        return [pltpu.VMEM(shape, dtype), pltpu.VMEM(shape, dtype)]

    dma = pltpu.SemaphoreType.DMA
    smem = pl.BlockSpec(memory_space=pltpu.SMEM)
    hbm = pl.BlockSpec(memory_space=pltpu.HBM)
    vmem = pl.BlockSpec(memory_space=pltpu.VMEM)
    scratch = [
        pltpu.SMEM(block_tenant.shape, jnp.int32),
        pltpu.SMEM(block_tenant.shape, jnp.int32),
        pltpu.SMEM(tenant_tokens.shape, jnp.int32),
        pltpu.SMEM(tenant_owner.shape, jnp.int32),
        pltpu.VMEM(hidden_in.shape, BF16),
        pltpu.VMEM(grad_gate.shape, BF16),
        pair((SIDE, SIDE, OWN, R, hd), BF16),
        pair((SIDE, SIDE, OWN, R, hf), BF16),
        pltpu.VMEM((BLK, R, ROWS), F32),
        pltpu.VMEM((BLK, R, ROWS), F32),
        pltpu.VMEM((n_tensor, bt, R, ROWS), F32),
        pltpu.VMEM((n_tensor, bt, R, ROWS), F32),
        pltpu.VMEM((BLK, R, ROWS), BF16),
        pltpu.VMEM((BLK, R, ROWS), BF16),
        pair((SIDE, BLK, R, hd), BF16),
        pair((SIDE, BLK, R, hf), BF16),
        pair((wide, SIDE * BLK * R), BF16),
        pair((wide, hd), F32),
        pair((wide, hf), F32),
        pair((SIDE, OWN * R, hd), BF16),
        pair((SIDE, OWN * R, hf), BF16),
        pair((SIDE - 1, OWN * R, hd), BF16),
        pair((SIDE - 1, OWN * R, hf), BF16),
        pltpu.VMEM((GROUPS, 2, R, ROWS), BF16),
        pltpu.VMEM((GROUPS, 2, R, ROWS), BF16),
        pltpu.VMEM((8, 128), F32),
        pltpu.VMEM((n_tensor, 8, 128), F32),
        pltpu.SMEM((BLK,), jnp.int32),
        pltpu.SMEM((2 * GROUPS,), jnp.int32),
        dma((24,)),
        dma((24, 3)),
        dma((4,)),
        dma((4,)),
        dma((2,)),
        dma((4,)),
        dma((4,)),
        dma((2,)),
        dma((10,)),
    ]
    results = pl.pallas_call(
        functools.partial(kernel, n_tensor),
        out_shape=(
            jax.ShapeDtypeStruct((GROUPS * 2 * ROWS, cd), BF16),
            jax.ShapeDtypeStruct((OWN, R, cd), F32),
            jax.ShapeDtypeStruct((OWN, R, cf), F32),
            jax.ShapeDtypeStruct((8, 128), F32),
        ),
        in_specs=[hbm] * 8,
        out_specs=(vmem,) * 4,
        scratch_shapes=scratch,
        compiler_params=pltpu.CompilerParams(
            collective_id=0, has_side_effects=True, vmem_limit_bytes=40 * 1024 * 1024
        ),
    )(
        *(
            pltpu.with_memory_space_constraint(a, pltpu.HBM)
            for a in (
                block_tenant,
                block_dest.reshape(-1),
                tenant_tokens,
                tenant_owner,
                hidden_in,
                grad_gate,
                adapter_in,
                adapter_out,
            )
        )
    )
    return pl.pallas_call(
        place,
        out_shape=(
            jax.ShapeDtypeStruct((GROUPS * 2 * ROWS, cd), BF16),
            jax.ShapeDtypeStruct((OWN, R, cd), F32),
            jax.ShapeDtypeStruct((OWN, R, cf), F32),
            jax.ShapeDtypeStruct((OWN,), F32),
        ),
        in_specs=[vmem, vmem, vmem, smem],
        out_specs=(hbm, hbm, hbm, smem),
        scratch_shapes=[dma((6,))],
        compiler_params=pltpu.CompilerParams(vmem_limit_bytes=16 * 1024 * 1024),
    )(*results)


def solution(mesh):
    return jax.shard_map(
        per_device,
        mesh=mesh,
        in_specs=(
            P("dp", "tensor"),
            P("dp", "tensor"),
            P("dp", None, "tensor"),
            P("dp", None, "tensor"),
            P(),
            P(),
            P(),
            P(),
        ),
        out_specs=(P("dp", "tensor"), P("dp", None, "tensor"), P("dp", None, "tensor"), P("dp")),
        check_vma=False,
    )
```

```python
import functools

import jax
import jax.numpy as jnp
from jax import lax
from jax.experimental import pallas as pl
from jax.experimental.pallas import tpu as pltpu
from jax.sharding import PartitionSpec as P

SIDE = 4
R = 16
ROWS = 128
BLK = 16
OWN = 4
GROUPS = SIDE * SIDE
MESH = pl.DeviceIdType.MESH
BF16 = jnp.bfloat16
F32 = jnp.float32


def remote(src, dst, send_sem, recv_sem, device):
    return pltpu.make_async_remote_copy(
        src_ref=src,
        dst_ref=dst,
        send_sem=send_sem,
        recv_sem=recv_sem,
        device_id=device,
        device_id_type=MESH,
    )


def await_bytes(ref, sem):
    pltpu.make_async_copy(ref, ref, sem).wait()


class Gather:
    def __init__(self, buf, first, second, ring, number, src):
        a, b = first[0], second[0]
        column = [buf.at[:, (a + k) % SIDE] for k in (0, 3, 1, 2)]
        row = ring(number, buf.at[b], first, src, True)
        mine = ring(number + 1, column[0], second, src, False)
        before, after, far = [ring(number + 1 + k, column[k], second, None, False) for k in (1, 2, 3)]

        def come(way, onward):
            def step():
                row.forward_one(way)
                onward.start()

            return step

        def opposite():
            row.finish()
            far.start()

        self.steps = [
            [row.start, mine.start],
            [come(0, before), come(1, after), opposite, mine.forward],
            [before.forward, after.forward],
            [far.forward, mine.finish],
            [before.finish, after.finish, far.finish],
        ]
        self.rings = (row, mine, before, after, far)

    def drain(self):
        for r in self.rings:
            r.drain()


class Ring:
    def __init__(self, buf, here, right, left, far, sends, recvs, src=None, direct=False):
        self.buf, self.here, self.right, self.left = buf, here, right, left
        half = buf.shape[1] // 2
        before, after = (here + 3) % SIDE, (here + 1) % SIDE
        own = buf.at[here] if src is None else src
        mine = buf.at[here]
        self.sends, self.recvs = sends, recvs
        self.own = [
            remote(own, mine, sends, recvs.at[0], right),
            remote(own, mine, sends, recvs.at[1], left),
        ]
        low = buf.at[before, pl.ds(0, half)]
        high = buf.at[after, pl.ds(half, half)]
        self.pass_on = [
            remote(low, low, sends, recvs.at[2], right),
            remote(high, high, sends, recvs.at[2], left),
        ]
        self.direct = direct
        if direct:
            self.own.append(remote(own, mine, sends, recvs.at[2], far))

    def start(self):
        for copy in self.own:
            copy.start()

    def forward_one(self, way):
        self.own[way].wait_recv()
        if not self.direct:
            self.pass_on[way].start()

    def forward(self):
        self.forward_one(0)
        self.forward_one(1)

    def finish(self):
        await_bytes(self.buf.at[(self.here + 2) % SIDE], self.recvs.at[2])

    def drain(self):
        await_bytes(self.buf.at[pl.ds(0, SIDE - 1)], self.sends)


def kernel(
    n_tensor,
    tenant_hbm,
    dest_hbm,
    tokens_hbm,
    owner_hbm,
    x_hbm,
    g_hbm,
    ain_hbm,
    aout_hbm,
    dg_v,
    gin_v,
    gout_v,
    norm_ref,
    tenant_ref,
    dest_ref,
    tokens_ref,
    owner_ref,
    x_v,
    g_v,
    tab_in,
    tab_out,
    low_part,
    fac_part,
    low_got,
    fac_got,
    low_all,
    fac_all,
    term_in,
    term_out,
    pick,
    sum_in,
    sum_out,
    to_in,
    to_out,
    from_in,
    from_out,
    slot_send,
    slots,
    sq_own,
    sq_got,
    pos_own,
    pos_slot,
    ring_s,
    ring_r,
    z_s,
    z_r,
    slot_sem,
    own_s,
    own_r,
    sq_sem,
    loc,
):
    me = lax.axis_index("dp")
    t = lax.axis_index("tensor")
    y, x = me // SIDE, me % SIDE
    bt = BLK // n_tensor
    cd, cf = x_v.shape[1], g_v.shape[1]
    hd, hf = cd // 2, cf // 2

    ends = []

    def at_dp(yy, xx):
        return {"dp": yy * SIDE + xx}

    x_right, x_left = at_dp(y, (x + 1) % SIDE), at_dp(y, (x + 3) % SIDE)
    y_right, y_left = at_dp((y + 1) % SIDE, x), at_dp((y + 3) % SIDE, x)
    x_far, y_far = at_dp(y, (x + 2) % SIDE), at_dp((y + 2) % SIDE, x)
    along_x, along_y = (x, x_right, x_left, x_far), (y, y_right, y_left, y_far)

    load_x = pltpu.make_async_copy(x_hbm, x_v, loc.at[8])
    load_g = pltpu.make_async_copy(g_hbm, g_v, loc.at[9])
    in_cols = [ain_hbm.at[:, :, pl.ds(h * hd, hd)] for h in range(2)]
    out_cols = [aout_hbm.at[:, :, pl.ds(h * hf, hf)] for h in range(2)]
    places = [(y, x), (x, y)]
    own_tables = []
    for h in range(2):
        own_tables.append(
            pltpu.make_async_copy(in_cols[h], tab_in[h].at[places[h][0], places[h][1]], loc.at[2 + h])
        )
        own_tables.append(
            pltpu.make_async_copy(
                out_cols[h], tab_out[h].at[places[h][0], places[h][1]], loc.at[4 + h]
            )
        )
    plan = [
        pltpu.make_async_copy(tenant_hbm, tenant_ref, loc.at[0]),
        pltpu.make_async_copy(owner_hbm, owner_ref, loc.at[1]),
        pltpu.make_async_copy(dest_hbm, dest_ref, loc.at[6]),
        pltpu.make_async_copy(tokens_hbm, tokens_ref, loc.at[7]),
    ]
    for copy in plan + own_tables:
        copy.start()
    load_x.start()
    load_g.start()

    barrier = pltpu.get_barrier_semaphore()

    def greet_dp(k, _):
        pl.semaphore_signal(
            barrier, inc=1, device_id={"dp": (me + k) % GROUPS}, device_id_type=MESH
        )
        return 0

    def greet_tensor(k, _):
        pl.semaphore_signal(
            barrier, inc=1, device_id={"tensor": (t + k) % n_tensor}, device_id_type=MESH
        )
        return 0

    lax.fori_loop(1, GROUPS, greet_dp, 0)
    lax.fori_loop(1, n_tensor, greet_tensor, 0)

    def place_of(block):
        return owner_ref[tenant_ref[block]]

    def own_places(b, _):
        pos_own[b] = place_of(me * BLK + b)
        return 0

    for copy in plan:
        copy.wait()
    lax.fori_loop(0, BLK, own_places, 0)
    pl.semaphore_wait(barrier, GROUPS - 1 + n_tensor - 1)

    def slot_places(s, _):
        one, two = jnp.int32(-1), jnp.int32(-1)
        for i in range(BLK):
            b = s * BLK + i
            hit = dest_ref[b] == me
            p = place_of(b)
            two = jnp.where(hit & (one >= 0), p, two)
            one = jnp.where(hit & (one < 0), p, one)
        pos_slot[2 * s] = jnp.maximum(one, 0)
        pos_slot[2 * s + 1] = jnp.maximum(two, 0)
        return 0

    def slot_tables():
        lax.fori_loop(0, GROUPS, slot_places, 0)

    def choose(q, _):
        lane = lax.broadcasted_iota(jnp.int32, (8, 128), 1)
        wide = (SIDE * OWN * R, 128)
        row = lax.broadcasted_iota(jnp.int32, wide, 0)
        same = (row & (R - 1)) == (lax.broadcasted_iota(jnp.int32, wide, 1) & (R - 1))
        tall = row >> 4
        g, first_blk = q // 2, (q % 2) * 8
        for h in range(2):
            group = y * SIDE + g if h == 0 else g * SIDE + x
            want = jnp.full((8, 128), -1, jnp.int32)
            for i in range(8):
                p = place_of(group * BLK + first_blk + i)
                if h == 0:
                    local = jnp.where(((p >> 2) & 3) == x, ((p >> 4) << 2) | (p & 3), -1)
                else:
                    local = jnp.where((p >> 4) == y, p & 15, -1)
                want = jnp.where((lane >> 4) == i, local, want)
            hit = (tall == want[0:1]) & same
            pick[h][:, pl.ds(pl.multiple_of(q * 128, 128), 128)] = jnp.where(hit, 1.0, 0.0).astype(BF16)
        return 0

    def choose_all():
        lax.fori_loop(0, 2 * SIDE, choose, 0)

    def find(k, found):
        at = owner_ref[k] - me * OWN
        return tuple(jnp.where(at == j, tokens_ref[k], found[j]) for j in range(OWN))

    def owned_weights():
        found = lax.fori_loop(0, owner_ref.shape[0], find, (jnp.int32(1),) * OWN)
        return [1.0 / jnp.full((1, 128), f, jnp.int32).astype(F32) for f in found]

    def ring(number, buf, along, src=None, direct=False):
        return Ring(buf, *along, ring_s.at[number], ring_r.at[number], src, direct)

    first, second = [along_x, along_y], [along_y, along_x]
    tab_in_ag = [Gather(tab_in[h], first[h], second[h], ring, 5 * h, in_cols[h]) for h in range(2)]
    tab_out_ag = [
        Gather(tab_out[h], first[h], second[h], ring, 10 + 5 * h, out_cols[h]) for h in range(2)
    ]

    def deep(gathers, depth):
        for part in range(len(gathers[0].steps[depth])):
            for gather in gathers:
                gather.steps[depth][part]()

    def partial_products(table, rows_v, half, part):
        def one(b, _):
            p = pos_own[b]
            rows = rows_v[pl.ds(pl.multiple_of(b * ROWS, ROWS), ROWS), :]
            tab_a = table[0][p >> 4, (p >> 2) & 3, p & 3]
            tab_b = table[1][(p >> 2) & 3, p >> 4, p & 3]
            nt = (((1,), (1,)), ((), ()))
            part[b] = lax.dot_general(
                tab_a, rows[:, :half], nt, preferred_element_type=F32
            ) + lax.dot_general(tab_b, rows[:, half:], nt, preferred_element_type=F32)
            return 0

        lax.fori_loop(0, BLK, one, 0, unroll=2)

    def reduce_copy(part, got, number, k):
        to = (t + k) % n_tensor
        return remote(
            part.at[pl.ds(to * bt, bt)],
            got.at[k],
            z_s.at[number],
            z_r.at[number],
            {"tensor": to},
        )

    def spread_copy(full, number, k):
        mine = full.at[pl.ds(t * bt, bt)]
        return remote(
            mine, mine, z_s.at[number], z_r.at[number], {"tensor": (t + k) % n_tensor}
        )

    def over_tensor(do):
        lax.fori_loop(1, n_tensor, lambda k, _: (do(k), 0)[1], 0, unroll=5)

    def send_parts(part, got, number):
        over_tensor(lambda k: reduce_copy(part, got, number, k).start())
        ends.append(lambda: await_bytes(got.at[pl.ds(1, n_tensor - 1)], z_s.at[number]))

    def add_parts(part, got, full, number, scale):
        await_bytes(got.at[pl.ds(1, n_tensor - 1)], z_r.at[number])
        total = lax.fori_loop(1, n_tensor, lambda k, acc: acc + got[k], part[pl.ds(t * bt, bt)], unroll=5)
        full[pl.ds(t * bt, bt)] = (scale * total).astype(BF16)
        over_tensor(lambda k: spread_copy(full, number + 1, k).start())
        ends.append(lambda: await_bytes(full.at[pl.ds(0, BLK - bt)], z_s.at[number + 1]))

    def take_spread(full, number):
        await_bytes(full.at[pl.ds(0, BLK - bt)], z_r.at[number])

    def terms(h, factor, rows_v, half, out):
        def one(b, _):
            rows = rows_v[pl.ds(pl.multiple_of(b * ROWS, ROWS), ROWS), pl.ds(h * half, half)]
            out[h][first[h][0], b] = jnp.dot(
                factor[b], rows, preferred_element_type=F32
            ).astype(BF16)
            return 0

        lax.fori_loop(0, BLK, one, 0, unroll=2)

    for gathers in (tab_in_ag, tab_out_ag):
        ends.extend(g.drain for g in gathers)
    deep(tab_in_ag, 0)
    deep(tab_out_ag, 0)
    slot_tables()
    deep(tab_in_ag, 1)
    deep(tab_in_ag, 2)
    deep(tab_in_ag, 3)
    deep(tab_in_ag, 4)
    for copy in own_tables:
        copy.wait()
    load_x.wait()
    partial_products(tab_in, x_v, hd, low_part)
    send_parts(low_part, low_got, 0)
    deep(tab_out_ag, 1)
    deep(tab_out_ag, 2)
    choose_all()
    add_parts(low_part, low_got, low_all, 0, 1.0)
    deep(tab_out_ag, 3)
    deep(tab_out_ag, 4)
    load_g.wait()
    partial_products(tab_out, g_v, hf, fac_part)
    send_parts(fac_part, fac_got, 2)
    take_spread(low_all, 1)
    term_out_1 = [ring(20 + h, term_out[h], first[h], None, False) for h in range(2)]
    for h in range(2):
        terms(h, low_all, g_v, hf, term_out)
        term_out_1[h].start()
        ends.append(term_out_1[h].drain)
    add_parts(fac_part, fac_got, fac_all, 2, 2.0)
    for r in term_out_1:
        r.forward()
    weight = owned_weights()
    take_spread(fac_all, 3)
    term_in_1 = [ring(22 + h, term_in[h], first[h], None, False) for h in range(2)]
    for h in range(2):
        terms(h, fac_all, x_v, hd, term_in)
        term_in_1[h].start()
        ends.append(term_in_1[h].drain)

    def slot_copy(k):
        to = (me + k) % GROUPS
        return remote(slot_send.at[k], slots.at[me], slot_sem.at[0], slot_sem.at[1], {"dp": to})

    def blocks_for(group):
        one, two = jnp.int32(-1), jnp.int32(-1)
        for i in range(BLK):
            hit = dest_ref[me * BLK + i] == group
            two = jnp.where(hit & (one >= 0), i, two)
            one = jnp.where(hit & (one < 0), i, one)
        return one, two

    def masked(i):
        live = jnp.where(i >= 0, 1.0, 0.0).astype(F32)
        return (fac_all[jnp.maximum(i, 0)].astype(F32) * live).astype(BF16)

    def pack(k, _):
        one, two = blocks_for((me + k) % GROUPS)
        slot_send[k, 0] = masked(one)
        slot_send[k, 1] = masked(two)
        slot_copy(k).start()
        return 0

    def owner_copies(number, h, sends, lands):
        here = second[h][0]
        copies = []
        for k in range(1, SIDE):
            to = (here + k) % SIDE
            device = at_dp(to, x) if h == 0 else at_dp(y, to)
            copies.append(
                remote(
                    sends.at[to],
                    lands.at[k - 1],
                    own_s.at[number],
                    own_r.at[number],
                    device,
                )
            )
        return copies

    def add_terms(h, term, total, sends):
        cols = total.shape[1]
        step = min(cols, 256)
        rows = SIDE * OWN * R

        def one(c, _):
            where = pl.ds(pl.multiple_of(c * step, step), step)
            block = term[:, :, :, where].reshape(SIDE * BLK * R, step)
            out = jnp.dot(pick[h][...], block, preferred_element_type=F32)
            total[:, where] = out
            sends[:, :, where] = out.reshape(SIDE, OWN * R, step).astype(BF16)
            return 0

        lax.fori_loop(0, cols // step, one, 0)

    def own_sum(h, total, lands, result, scale, half):
        here = second[h][0]
        kept = total[pl.ds(pl.multiple_of(here * OWN * R, OWN * R), OWN * R), :]
        for k in range(SIDE - 1):
            kept = kept + lands[k].astype(F32)
        squares = []
        for j in range(OWN):
            piece = kept[j * R : (j + 1) * R] * scale[j]
            result[j, :, pl.ds(h * half, half)] = piece
            squares.append(jnp.sum(piece * piece, axis=0, keepdims=True))
        return squares

    out_own = [owner_copies(h, h, to_out[h], from_out[h]) for h in range(2)]
    in_own = [owner_copies(2 + h, h, to_in[h], from_in[h]) for h in range(2)]
    for h in range(2):
        term_out_1[h].finish()
        add_terms(h, term_out[h], sum_out[h], to_out[h])
    for r in term_in_1:
        r.forward()
    lax.fori_loop(1, GROUPS, pack, 0)

    ends.append(lambda: await_bytes(slots.at[pl.ds(0, GROUPS - 1)], slot_sem.at[0]))
    one, two = blocks_for(me)
    slots[me, 0] = masked(one)
    slots[me, 1] = masked(two)

    for h in range(2):
        for copy in out_own[h]:
            copy.start()

    for h in range(2):
        term_in_1[h].finish()
        add_terms(h, term_in[h], sum_in[h], to_in[h])
        for copy in in_own[h]:
            copy.start()

    await_bytes(slots.at[pl.ds(0, GROUPS - 1)], slot_sem.at[1])

    def apply_factor(i, _):
        p = pos_slot[i]
        factor = slots[i // 2, i % 2]
        rows = pl.ds(pl.multiple_of(i * ROWS, ROWS), ROWS)
        tn = (((0,), (0,)), ((), ()))
        dg_v[rows, :hd] = lax.dot_general(
            factor, tab_in[0][p >> 4, (p >> 2) & 3, p & 3], tn, preferred_element_type=F32
        ).astype(BF16)
        dg_v[rows, hd:] = lax.dot_general(
            factor, tab_in[1][(p >> 2) & 3, p >> 4, p & 3], tn, preferred_element_type=F32
        ).astype(BF16)
        return 0

    lax.fori_loop(0, 2 * GROUPS, apply_factor, 0, unroll=4)

    def weigh(half, by):
        return [jnp.tile(by * w, (1, half // 128)) for w in weight]

    for h in range(2):
        await_bytes(from_out[h], own_r.at[h])
    parts = [own_sum(h, sum_out[h], from_out[h], gout_v, weigh(hf, 2.0), hf) for h in range(2)]
    for h in range(2):
        await_bytes(from_in[h], own_r.at[2 + h])
    parts += [own_sum(h, sum_in[h], from_in[h], gin_v, weigh(hd, 1.0), hd) for h in range(2)]

    for h in range(2):
        ends.append(functools.partial(await_bytes, from_out[h], own_s.at[h]))
        ends.append(functools.partial(await_bytes, from_in[h], own_s.at[2 + h]))

    row8 = lax.broadcasted_iota(jnp.int32, (8, 128), 0)
    square = jnp.zeros((8, 128), F32)
    for j in range(OWN):
        one_sum = jnp.zeros((1, 128), F32)
        for part in parts:
            for c in range(part[j].shape[1] // 128):
                one_sum = one_sum + part[j][:, c * 128 : (c + 1) * 128]
        square = jnp.where(row8 == j, one_sum, square)
    sq_own[...] = square

    def square_copy(k):
        return remote(
            sq_own, sq_got.at[k], sq_sem.at[0], sq_sem.at[1], {"tensor": (t + k) % n_tensor}
        )

    over_tensor(lambda k: square_copy(k).start())
    ends.append(lambda: await_bytes(sq_got.at[pl.ds(1, n_tensor - 1)], sq_sem.at[0]))
    await_bytes(sq_got.at[pl.ds(1, n_tensor - 1)], sq_sem.at[1])
    total = lax.fori_loop(1, n_tensor, lambda k, acc: acc + sq_got[k], sq_own[...], unroll=5)
    norm_ref[...] = jnp.sqrt(jnp.broadcast_to(jnp.sum(total, axis=1, keepdims=True), (8, 128)))

    for end in ends:
        end()


def place(dg, gin, gout, norms, dg_to, gin_to, gout_to, norms_to, sems):
    quarter = dg.shape[0] // 4
    moves = [(gin, gin_to), (gout, gout_to)]
    for i in range(4):
        rows = pl.ds(i * quarter, quarter)
        moves.append((dg.at[rows], dg_to.at[rows]))
    copies = [pltpu.make_async_copy(a, b, sems.at[i]) for i, (a, b) in enumerate(moves)]
    for copy in copies:
        copy.start()
    for j in range(OWN):
        norms_to[j] = norms[j, 0]
    for copy in copies:
        copy.wait()


def per_device(
    hidden_in, grad_gate, adapter_in, adapter_out, block_tenant, block_dest, tenant_tokens, tenant_owner
):
    n_tensor = lax.axis_size("tensor")
    bt = BLK // n_tensor
    cd, cf = hidden_in.shape[1], grad_gate.shape[1]
    hd, hf = cd // 2, cf // 2
    wide = SIDE * OWN * R

    def pair(shape, dtype):
        return [pltpu.VMEM(shape, dtype), pltpu.VMEM(shape, dtype)]

    dma = pltpu.SemaphoreType.DMA
    smem = pl.BlockSpec(memory_space=pltpu.SMEM)
    hbm = pl.BlockSpec(memory_space=pltpu.HBM)
    vmem = pl.BlockSpec(memory_space=pltpu.VMEM)
    scratch = [
        pltpu.SMEM(block_tenant.shape, jnp.int32),
        pltpu.SMEM(block_tenant.shape, jnp.int32),
        pltpu.SMEM(tenant_tokens.shape, jnp.int32),
        pltpu.SMEM(tenant_owner.shape, jnp.int32),
        pltpu.VMEM(hidden_in.shape, BF16),
        pltpu.VMEM(grad_gate.shape, BF16),
        pair((SIDE, SIDE, OWN, R, hd), BF16),
        pair((SIDE, SIDE, OWN, R, hf), BF16),
        pltpu.VMEM((BLK, R, ROWS), F32),
        pltpu.VMEM((BLK, R, ROWS), F32),
        pltpu.VMEM((n_tensor, bt, R, ROWS), F32),
        pltpu.VMEM((n_tensor, bt, R, ROWS), F32),
        pltpu.VMEM((BLK, R, ROWS), BF16),
        pltpu.VMEM((BLK, R, ROWS), BF16),
        pair((SIDE, BLK, R, hd), BF16),
        pair((SIDE, BLK, R, hf), BF16),
        pair((wide, SIDE * BLK * R), BF16),
        pair((wide, hd), F32),
        pair((wide, hf), F32),
        pair((SIDE, OWN * R, hd), BF16),
        pair((SIDE, OWN * R, hf), BF16),
        pair((SIDE - 1, OWN * R, hd), BF16),
        pair((SIDE - 1, OWN * R, hf), BF16),
        pltpu.VMEM((GROUPS, 2, R, ROWS), BF16),
        pltpu.VMEM((GROUPS, 2, R, ROWS), BF16),
        pltpu.VMEM((8, 128), F32),
        pltpu.VMEM((n_tensor, 8, 128), F32),
        pltpu.SMEM((BLK,), jnp.int32),
        pltpu.SMEM((2 * GROUPS,), jnp.int32),
        dma((24,)),
        dma((24, 3)),
        dma((4,)),
        dma((4,)),
        dma((2,)),
        dma((4,)),
        dma((4,)),
        dma((2,)),
        dma((10,)),
    ]
    results = pl.pallas_call(
        functools.partial(kernel, n_tensor),
        out_shape=(
            jax.ShapeDtypeStruct((GROUPS * 2 * ROWS, cd), BF16),
            jax.ShapeDtypeStruct((OWN, R, cd), F32),
            jax.ShapeDtypeStruct((OWN, R, cf), F32),
            jax.ShapeDtypeStruct((8, 128), F32),
        ),
        in_specs=[hbm] * 8,
        out_specs=(vmem,) * 4,
        scratch_shapes=scratch,
        compiler_params=pltpu.CompilerParams(
            collective_id=0, has_side_effects=True, vmem_limit_bytes=40 * 1024 * 1024
        ),
    )(
        *(
            pltpu.with_memory_space_constraint(a, pltpu.HBM)
            for a in (
                block_tenant,
                block_dest.reshape(-1),
                tenant_tokens,
                tenant_owner,
                hidden_in,
                grad_gate,
                adapter_in,
                adapter_out,
            )
        )
    )
    return pl.pallas_call(
        place,
        out_shape=(
            jax.ShapeDtypeStruct((GROUPS * 2 * ROWS, cd), BF16),
            jax.ShapeDtypeStruct((OWN, R, cd), F32),
            jax.ShapeDtypeStruct((OWN, R, cf), F32),
            jax.ShapeDtypeStruct((OWN,), F32),
        ),
        in_specs=[vmem, vmem, vmem, smem],
        out_specs=(hbm, hbm, hbm, smem),
        scratch_shapes=[dma((6,))],
        compiler_params=pltpu.CompilerParams(vmem_limit_bytes=16 * 1024 * 1024),
    )(*results)


def solution(mesh):
    return jax.shard_map(
        per_device,
        mesh=mesh,
        in_specs=(
            P("dp", "tensor"),
            P("dp", "tensor"),
            P("dp", None, "tensor"),
            P("dp", None, "tensor"),
            P(),
            P(),
            P(),
            P(),
        ),
        out_specs=(P("dp", "tensor"), P("dp", None, "tensor"), P("dp", None, "tensor"), P("dp")),
        check_vma=False,
    )
```
